32 devices in a mesh: parts: 2 (over y), blk: 4 (over z), col: 4 (over x, core).
Axes of the slice: x: 2, y: 2, z: 4, core: 2. Of those that a mesh axis runs over, the one named last changes fastest.
Arguments:
- tiles: bfloat16 [8, 4, 4, 10, 128, 128], P(('parts', 'blk'), 'col'), parts along dimension 0
- tile_dest: int32 [8, 4, 4, 10], P(('parts', 'blk'), 'col'), parts along dimension 0, may hold values from 0 to 3
- tile_count: int32 [8, 4, 4], P(('parts', 'blk'), 'col'), parts along dimension 0, may hold values from 1 to 10, as said below
- topic_seeds: int32 [512, 64], P('parts'), parts along dimension 0, may hold values from 0 to 2047
Outputs:
- scores: float32 [4096, 256], P(('parts', 'blk', 'col')), parts along dimension 0
The draws below stay inside these ranges and needn't reach their ends.
There are 2 independent parts, one for each index of `parts`. The reference program is written for one: setup_inputs(seed, part) draws one part's arguments, and reference() takes and returns one part's arrays. A program takes and returns all parts, laid end to end along the dimension named above; each array names one. Nothing has to cross between parts.
Inputs may be any that keep to these rules, and one draw needn't show every extreme that they name: `tile_count`: live tiles of a group of slots; the largest value is 10 in every draw.
All inputs are finite; a program needn't handle non-finite values.
Results may differ from the reference program's by a relative error of at most 0.01.
Values may be sent and summed in bfloat16 or wider, within the bound.
No kernel may reach another device: no remote copies, remote signals or barrier semaphores. Data moves between devices by JAX's collectives and lax.ppermute only.
A program may use at most 64 MiB of HBM per device.

```python
import math
import jax
import jax.numpy as jnp
from jax import lax

TILE = 128
TOPICS = 256
SEEDS = 64
TPS = 10
ITERS = 3
HOSTS = 2048
N_BLK = 4
N_COL = 4


def draw_tiles(key, part):
    key = jax.random.fold_in(key, 11)
    arc_key, hub_key = jax.random.split(key)
    uniform_draw = jax.random.uniform(arc_key, (N_BLK, N_COL, N_BLK, TPS, TILE, TILE), jnp.float32)
    keep_rate = 1.25 / TILE
    hub_low = 0.25
    hub_high = 4.0
    hub_table = jnp.exp(jax.random.uniform(hub_key, (N_BLK * N_COL, TILE), jnp.float32, math.log(hub_low), math.log(hub_high)))
    hub_mean = (hub_high - hub_low) / math.log(hub_high / hub_low)
    row_ids = jnp.arange(N_BLK, dtype=jnp.int32)[:, None, None]
    column_ids = jnp.arange(N_COL, dtype=jnp.int32)[None, :, None]
    step_ids = jnp.arange(N_BLK, dtype=jnp.int32)[None, None, :]
    source_block = (row_ids - step_ids) % N_BLK * N_COL + column_ids
    hub_weight = hub_table[source_block][:, :, :, None, None, :]
    arc_level = jnp.clip(uniform_draw / keep_rate, 0.0, 1.0)
    arc_value = jnp.exp(math.log(0.001) * (1.0 - arc_level))
    value_mean = (1.0 - 0.001) / math.log(1000.0)
    weights = jnp.where(uniform_draw < keep_rate, arc_value, 0.0) * hub_weight
    normaliser = 1.0 / (1.25 * N_BLK * (TPS + 1) * 0.5 * value_mean * hub_mean)
    return (weights * normaliser).astype(jnp.bfloat16)


def draw_tile_count(key, part):
    key = jax.random.fold_in(key, 7)
    first_key, second_key = jax.random.split(key)
    base_counts = jax.random.randint(first_key, (N_BLK, N_COL, N_BLK), 1, TPS + 1)
    hub_row = jax.random.randint(second_key, (), 0, N_BLK)
    row_ids = jnp.arange(N_BLK, dtype=jnp.int32)[:, None, None]
    return jnp.where(row_ids == hub_row, TPS, base_counts).astype(jnp.int32)


def plant(values, rng, low, top_value):
    dims = values.shape
    place = [jax.random.randint(jax.random.fold_in(rng, axis), (), 0, dims[axis]) for axis in range(len(dims))]
    values = values.at[tuple(place)].set(low)
    longest = dims.index(max(dims))
    place[longest] = (place[longest] + 1) % dims[longest]
    return values.at[tuple(place)].set(top_value)


def setup_inputs(seed: int = 0, part: int = 0) -> dict:
    key_of = jax.random.split(jax.random.key(seed), 5)
    own_keys = jax.random.split(jax.random.fold_in(key_of[4], part), 5)
    tiles = draw_tiles(jax.random.fold_in(jax.random.fold_in(key_of[4], part), 71), part)
    tile_dest = plant(jax.random.randint(own_keys[1], (N_BLK, N_COL, N_BLK, TPS), 0, N_COL), jax.random.fold_in(own_keys[1], 1), 0, N_COL - 1).astype(jnp.int32)
    tile_count = draw_tile_count(jax.random.fold_in(jax.random.fold_in(key_of[4], part), 71), part)
    topic_seeds = plant(jax.random.randint(own_keys[3], (TOPICS, SEEDS), 0, HOSTS), jax.random.fold_in(own_keys[3], 1), 0, HOSTS - 1).astype(jnp.int32)
    return dict(tiles=tiles, tile_dest=tile_dest, tile_count=tile_count, topic_seeds=topic_seeds)


damping = 0.85


def reference(tiles, tile_dest, tile_count, topic_seeds):
    topic_index = jnp.arange(TOPICS, dtype=jnp.int32)[:, None]
    host_seeds = jnp.zeros((HOSTS, TOPICS), jnp.float32).at[topic_seeds, topic_index].add(1.0)
    restart = (HOSTS / SEEDS) * host_seeds
    slot_ids = jnp.arange(TPS, dtype=jnp.int32)
    block_ids = jnp.arange(N_COL, dtype=jnp.int32)
    scores = restart
    for iteration in range(ITERS):
        sent_blocks = scores.astype(jnp.bfloat16).reshape(N_BLK, N_COL, TILE, TOPICS)

        def block_row(row_index):
            def column_group(column_index):
                sources = (row_index - jnp.arange(N_BLK, dtype=jnp.int32)) % N_BLK
                held_blocks = sent_blocks[sources, column_index]
                group_tiles = tiles[row_index, column_index]
                products = jnp.einsum("stij,sjk->stik", group_tiles.astype(jnp.float32),
                                      held_blocks.astype(jnp.float32), precision=lax.Precision.HIGHEST)
                live_mask = slot_ids[None, :] < tile_count[row_index, column_index][:, None]
                placing = ((tile_dest[row_index, column_index][:, :, None] == block_ids[None, None, :])
                           & live_mask[:, :, None]).astype(jnp.float32)
                partial_value = jnp.einsum("std,stik->dik", placing, products, precision=lax.Precision.HIGHEST)
                return lax.optimization_barrier(partial_value.astype(jnp.bfloat16)).astype(jnp.float32)

            return jnp.sum(lax.map(column_group, jnp.arange(N_COL, dtype=jnp.int32)), axis=0)

        propagated = lax.map(block_row, jnp.arange(N_BLK, dtype=jnp.int32)).reshape(HOSTS, TOPICS)
        scores = damping * propagated + (1.0 - damping) * restart
    return scores
```

```python
import functools

import jax
import jax.numpy as jnp
from jax import lax
from jax.experimental import pallas as pl
from jax.experimental.pallas import tpu as pltpu
from jax.sharding import PartitionSpec as P

ITERS = 3
CORES = 2
FIELD = 8
PACKED = 4

damping = 0.85

VMEM = pl.BlockSpec(memory_space=pltpu.VMEM)
SMEM = pl.BlockSpec(memory_space=pltpu.SMEM)
HBM = pl.BlockSpec(memory_space=pltpu.HBM)
MIB = 1 << 20


def place():
    col = lax.axis_index("col")
    return lax.axis_index("blk"), col // CORES, col % CORES


def packed_counts(ids, weights, edge):
    seeds, lanes = ids.shape
    rows = lax.broadcasted_iota(jnp.int32, (edge, lanes), 0)

    def add_seed(j, total):
        hit = rows == ids[pl.ds(j, 1), :]
        return [t + jnp.where(hit, w[pl.ds(j, 1), :], 0) for t, w in zip(total, weights)]

    zero = jnp.zeros((edge, lanes), jnp.int32)
    return lax.fori_loop(0, seeds, add_seed, [zero for _ in weights], unroll=16)


def field(packed, index):
    return ((packed >> (FIELD * index)) & ((1 << FIELD) - 1)).astype(jnp.float32)


def first_kernel(
    steps, columns, scale, tiles, dest, count, seeds,
    dense, keep, send, seed_rows, tile_buf, seed_buf, total, ids, weights, tile_sem, seed_sem,
):
    slots, edge = tile_buf.shape[1], tile_buf.shape[2]
    topics = seed_buf.shape[1]
    row, chip, core = place()
    col = chip * CORES + core
    fetch_seeds = [
        pltpu.make_async_copy(
            seeds.at[pl.ds(lax.rem(core + h, CORES) * topics, topics), :], seed_buf.at[h], seed_sem.at[h]
        )
        for h in range(CORES)
    ]
    fetch_tiles = [
        pltpu.make_async_copy(tiles.at[0, 0, s], tile_buf.at[s], tile_sem.at[s]) for s in range(steps)
    ]
    for fetch in fetch_seeds + fetch_tiles:
        fetch.start()

    groups = -(-steps // PACKED)
    counts = []
    for h in range(CORES):
        fetch_seeds[h].wait()
        hosts = seed_buf[h].astype(jnp.float32).T.astype(jnp.int32)
        if h == 0:
            seed_rows[...] = hosts
        ids[h] = hosts & (edge - 1)
        block = hosts >> (edge.bit_length() - 1)
        step = lax.rem(row - block // columns + steps, steps)
        mine = lax.rem(block, columns) == col
        one = 1 << (FIELD * lax.rem(step, PACKED))
        for g in range(groups):
            weights[h, g] = jnp.where(mine & (step // PACKED == g), one, 0)
        counts.append(packed_counts(ids.at[h], [weights.at[h, g] for g in range(groups)], edge))
    restart = [
        jnp.concatenate(
            [scale * field(counts[h][s // PACKED], s % PACKED) for s in range(steps)], axis=0
        ).astype(jnp.bfloat16)
        for h in range(CORES)
    ]

    for s in range(steps):
        fetch_tiles[s].wait()
        total[...] = jnp.zeros_like(total)

        def add_tile(t, carry):
            rows = pl.ds(pl.multiple_of(dest[0, 0, s, t] * edge, edge), edge)
            total[rows, :] += tile_buf[s, t].astype(jnp.float32)
            return carry

        lax.fori_loop(0, count[0, 0, s], add_tile, 0)
        dense[:, s * edge : (s + 1) * edge] = total[...].astype(jnp.bfloat16)

    keep[...] = jnp.dot(dense[...], restart[0], preferred_element_type=jnp.float32)
    send[...] = jnp.dot(dense[...], restart[1], preferred_element_type=jnp.float32).astype(jnp.bfloat16)


def restart_kernel(columns, scale, seed_rows, restart, ids, weight):
    edge = restart.shape[0] // CORES
    row, chip, core = place()
    hosts = seed_rows[...]
    ids[...] = hosts & (edge - 1)
    block = hosts >> (edge.bit_length() - 1)
    offset = block - row * columns - chip * CORES
    weight[...] = jnp.where(
        (offset >= 0) & (offset < CORES), 1 << (FIELD * jnp.clip(offset, 0, CORES - 1)), 0
    )
    (packed,) = packed_counts(ids, [weight], edge)
    for c in range(CORES):
        restart[c * edge : (c + 1) * edge, :] = (1.0 - damping) * (scale * field(packed, c))


def split_kernel(chips, keep, recv, mine, *sends):
    _, chip, _ = place()
    size = mine.shape[0]
    for d in range(chips):
        rows = pl.ds(pl.multiple_of(lax.rem(chip + d, chips) * size, size), size)
        part = keep[rows, :] + recv[rows, :].astype(jnp.float32)
        if d == 0:
            mine[...] = part
        else:
            sends[d - 1][...] = part.astype(jnp.bfloat16)


def gathered(scores, core, edge):
    return [
        jnp.concatenate([s[pl.ds(pl.multiple_of(c * edge, edge), edge), :] for s in scores], axis=0)
        for c in (core, 1 - core)
    ]


def step_kernel(chips, steps, own, other, *refs):
    scores, mine, sends = refs[:steps], refs[steps], refs[steps + 1 :]
    _, chip, core = place()
    size = mine.shape[0]
    sources = gathered(scores, core, size // CORES)
    for d in [*range(1, chips), 0]:
        rows = pl.ds(pl.multiple_of(lax.rem(chip + d, chips) * size, size), size)
        part = jnp.dot(own[rows, :], sources[0], preferred_element_type=jnp.float32)
        part += jnp.dot(other[rows, :], sources[1], preferred_element_type=jnp.float32)
        if d == 0:
            mine[...] = part
        else:
            sends[d - 1][...] = part.astype(jnp.bfloat16)


def last_kernel(chips, steps, own, other, restart, *refs):
    scores, parts = refs[:steps], refs[steps:]
    _, chip, core = place()
    edge = parts[0].shape[0]
    sources = gathered(scores, core, edge)
    for d in range(chips):
        for e in range(CORES):
            owner = lax.rem(core + e, CORES)
            block = lax.rem(chip + d, chips) * CORES + owner
            rows = pl.ds(pl.multiple_of(block * edge, edge), edge)
            part = jnp.dot(own[rows, :], sources[0], preferred_element_type=jnp.float32)
            part += jnp.dot(other[rows, :], sources[1], preferred_element_type=jnp.float32)
            if d == 0:
                rows = pl.ds(pl.multiple_of(owner * edge, edge), edge)
                part = damping * part + restart[rows, :]
            ref = parts[d * CORES + e]
            ref[...] = part.astype(ref.dtype)


def final_kernel(chips, *refs):
    parts, out = refs[:-1], refs[-1]
    _, _, core = place()
    topics = parts[0].shape[1]
    for e in range(CORES):
        total = sum(parts[d * CORES + e][...].astype(jnp.float32) for d in range(1, chips))
        lanes = pl.ds(pl.multiple_of(lax.rem(core + e, CORES) * topics, topics), topics)
        out[:, lanes] = parts[e][...] + damping * total


def from_col(value, chips, chip_step, core_step):
    route = [
        (x * CORES + c, (x + chip_step) % chips * CORES + (c + core_step) % CORES)
        for x in range(chips)
        for c in range(CORES)
    ]
    return lax.ppermute(value, "col", route)


def from_blk(value, steps, distance):
    return lax.ppermute(value, "blk", [(i, (i + distance) % steps) for i in range(steps)])


def body(tiles, tile_dest, tile_count, topic_seeds):
    slots, edge = tiles.shape[3], tiles.shape[4]
    steps, columns = lax.axis_size("blk"), lax.axis_size("col")
    chips = columns // CORES
    topics, seeds = topic_seeds.shape[0] // CORES, topic_seeds.shape[1]
    dests, sources, pair = columns * edge, steps * edge, CORES * edge
    groups = -(-steps // PACKED)
    scale = steps * columns * edge / seeds
    f32, bf16, i32 = jnp.float32, jnp.bfloat16, jnp.int32

    def shape(dtype, *dims):
        return jax.ShapeDtypeStruct(dims, dtype)

    def call(kernel, in_specs, outs, room, scratch=()):
        return pl.pallas_call(
            kernel,
            in_specs=in_specs,
            out_shape=outs,
            out_specs=[VMEM] * len(outs),
            scratch_shapes=scratch,
            compiler_params=pltpu.CompilerParams(vmem_limit_bytes=room),
        )

    matrix = 2 * dests * sources
    dense, keep, send, seed_rows = call(
        functools.partial(first_kernel, steps, columns, scale),
        [HBM, SMEM, SMEM, HBM],
        [
            shape(bf16, dests, sources),
            shape(f32, dests, topics),
            shape(bf16, dests, topics),
            shape(i32, seeds, topics),
        ],
        6 * MIB + 2 * matrix + 2 * steps * slots * edge * edge,
        [
            pltpu.VMEM((steps, slots, edge, edge), bf16),
            pltpu.VMEM((CORES, topics, seeds), i32),
            pltpu.VMEM((dests, edge), f32),
            pltpu.VMEM((CORES, seeds, topics), i32),
            pltpu.VMEM((CORES, groups, seeds, topics), i32),
            pltpu.SemaphoreType.DMA((steps,)),
            pltpu.SemaphoreType.DMA((CORES,)),
        ],
    )(tiles, tile_dest, tile_count, topic_seeds)
    (restart,) = call(
        functools.partial(restart_kernel, columns, scale),
        [VMEM],
        [shape(f32, pair, topics)],
        4 * MIB,
        [pltpu.VMEM((seeds, topics), i32), pltpu.VMEM((seeds, topics), i32)],
    )(seed_rows)
    recv = from_col(send, chips, 0, 1)
    split = [shape(f32, pair, topics)] + [shape(bf16, pair, topics)] * (chips - 1)
    parts = call(functools.partial(split_kernel, chips), [VMEM] * 2, split, 6 * MIB)(keep, recv)

    other = from_col(dense, chips, 0, 1)
    for iteration in range(ITERS):
        if iteration:
            parts = call(
                functools.partial(step_kernel, chips, steps),
                [VMEM] * (2 + steps),
                split,
                6 * MIB + 2 * matrix,
            )(dense, other, *gather)
        total = parts[0]
        for d in range(1, chips):
            total = total + from_col(parts[d], chips, d, 0).astype(f32)
        sent = (damping * total + restart).astype(bf16)
        gather = [sent] + [from_blk(sent, steps, d) for d in range(1, steps)]
        if iteration == ITERS - 2:
            break
    parts = call(
        functools.partial(last_kernel, chips, steps),
        [VMEM] * (3 + steps),
        [shape(f32, edge, topics)] * CORES + [shape(bf16, edge, topics)] * (CORES * (chips - 1)),
        6 * MIB + 2 * matrix,
    )(dense, other, restart, *gather)
    arrived = [
        part if d == e == 0 else from_col(part, chips, d, e)
        for (d, e), part in zip([(d, e) for d in range(chips) for e in range(CORES)], parts)
    ]
    (out,) = call(
        functools.partial(final_kernel, chips),
        [VMEM] * len(arrived),
        [shape(f32, edge, CORES * topics)],
        4 * MIB,
    )(*arrived)
    return out


def solution(mesh):
    return jax.shard_map(
        body,
        mesh=mesh,
        in_specs=(
            P(("parts", "blk"), "col", None, None, None, None),
            P(("parts", "blk"), "col", None, None),
            P(("parts", "blk"), "col", None),
            P("parts", None),
        ),
        out_specs=P(("parts", "blk", "col"), None),
        check_vma=False,
    )
```

```python
import functools

import jax
import jax.numpy as jnp
from jax import lax
from jax.experimental import pallas as pl
from jax.experimental.pallas import tpu as pltpu
from jax.sharding import PartitionSpec as P

ITERS = 3
CORES = 2
FIELD = 8
PACKED = 4

damping = 0.85

VMEM = pl.BlockSpec(memory_space=pltpu.VMEM)
HBM = pl.BlockSpec(memory_space=pltpu.HBM)
MIB = 1 << 20


def place():
    col = lax.axis_index("col")
    return lax.axis_index("blk"), col // CORES, col % CORES


def packed_counts(ids, weights, edge):
    seeds, lanes = ids.shape
    rows = lax.broadcasted_iota(jnp.int32, (edge, lanes), 0)

    def add_seed(j, total):
        hit = rows == ids[pl.ds(j, 1), :]
        return [t + jnp.where(hit, w[pl.ds(j, 1), :], 0) for t, w in zip(total, weights)]

    zero = jnp.zeros((edge, lanes), jnp.int32)
    return lax.fori_loop(0, seeds, add_seed, [zero for _ in weights], unroll=16)


def field(packed, index):
    return ((packed >> (FIELD * index)) & ((1 << FIELD) - 1)).astype(jnp.float32)


def first_kernel(
    steps, columns, scale, tiles_hbm, dest_hbm, count_hbm, seeds_hbm,
    dense, keep, send, seed_rows,
    tiles, dest, count, seeds, total, ids, weights, tile_sem, table_sem,
):
    slots, edge = tiles.shape[1], tiles.shape[2]
    topics = seeds.shape[1] // CORES
    row, chip, core = place()
    col = chip * CORES + core
    tables = [(seeds_hbm, seeds), (dest_hbm, dest), (count_hbm, count)]
    fetch_tables = [
        pltpu.make_async_copy(source, table, table_sem.at[i]) for i, (source, table) in enumerate(tables)
    ]
    fetch_tiles = [
        pltpu.make_async_copy(tiles_hbm.at[0, 0, s], tiles.at[s], tile_sem.at[s]) for s in range(steps)
    ]
    for fetch in fetch_tables + fetch_tiles:
        fetch.start()

    groups = -(-steps // PACKED)
    counts = []
    fetch_tables[0].wait()
    for h in range(CORES):
        lanes = pl.ds(pl.multiple_of(lax.rem(core + h, CORES) * topics, topics), topics)
        hosts = seeds[:, lanes]
        if h == 0:
            seed_rows[...] = hosts
        ids[h] = hosts & (edge - 1)
        block = hosts >> (edge.bit_length() - 1)
        step = lax.rem(row - block // columns + steps, steps)
        mine = lax.rem(block, columns) == col
        one = 1 << (FIELD * lax.rem(step, PACKED))
        for g in range(groups):
            weights[h, g] = jnp.where(mine & (step // PACKED == g), one, 0)
        counts.append(packed_counts(ids.at[h], [weights.at[h, g] for g in range(groups)], edge))
    restart = [
        jnp.concatenate(
            [scale * field(counts[h][s // PACKED], s % PACKED) for s in range(steps)], axis=0
        ).astype(jnp.bfloat16)
        for h in range(CORES)
    ]

    for fetch in fetch_tables[1:]:
        fetch.wait()
    for s in range(steps):
        fetch_tiles[s].wait()
        total[...] = jnp.zeros_like(total)

        def add_tile(t, carry):
            rows = pl.ds(pl.multiple_of(dest[0, 0, s, t] * edge, edge), edge)
            total[rows, :] += tiles[s, t].astype(jnp.float32)
            return carry

        lax.fori_loop(0, count[0, 0, s], add_tile, 0)
        dense[:, s * edge : (s + 1) * edge] = total[...].astype(jnp.bfloat16)

    keep[...] = jnp.dot(dense[...], restart[0], preferred_element_type=jnp.float32)
    send[...] = jnp.dot(dense[...], restart[1], preferred_element_type=jnp.float32).astype(jnp.bfloat16)


def restart_kernel(columns, scale, seed_rows, restart, ids, weight):
    edge = restart.shape[0] // CORES
    row, chip, core = place()
    hosts = seed_rows[...]
    ids[...] = hosts & (edge - 1)
    block = hosts >> (edge.bit_length() - 1)
    offset = block - row * columns - chip * CORES
    weight[...] = jnp.where(
        (offset >= 0) & (offset < CORES), 1 << (FIELD * jnp.clip(offset, 0, CORES - 1)), 0
    )
    (packed,) = packed_counts(ids, [weight], edge)
    for c in range(CORES):
        restart[c * edge : (c + 1) * edge, :] = (1.0 - damping) * (scale * field(packed, c))


def split_kernel(chips, keep, recv, mine, *sends):
    _, chip, _ = place()
    size = mine.shape[0]
    for d in range(chips):
        rows = pl.ds(pl.multiple_of(lax.rem(chip + d, chips) * size, size), size)
        part = keep[rows, :] + recv[rows, :].astype(jnp.float32)
        if d == 0:
            mine[...] = part
        else:
            sends[d - 1][...] = part.astype(jnp.bfloat16)


def gathered(scores, core, edge):
    return [
        jnp.concatenate([s[pl.ds(pl.multiple_of(c * edge, edge), edge), :] for s in scores[::-1]], axis=0)
        for c in (core, 1 - core)
    ]


def step_kernel(chips, steps, own, other, *refs):
    scores, mine, sends = refs[:steps], refs[steps], refs[steps + 1 :]
    _, chip, core = place()
    size = mine.shape[0]
    sources = gathered(scores, core, size // CORES)
    for d in [*range(1, chips), 0]:
        rows = pl.ds(pl.multiple_of(lax.rem(chip + d, chips) * size, size), size)
        part = jnp.dot(own[rows, :], sources[0], preferred_element_type=jnp.float32)
        part += jnp.dot(other[rows, :], sources[1], preferred_element_type=jnp.float32)
        if d == 0:
            mine[...] = part
        else:
            sends[d - 1][...] = part.astype(jnp.bfloat16)


def last_kernel(chips, steps, own, other, restart, *refs):
    scores, parts = refs[:steps], refs[steps:]
    _, chip, core = place()
    edge = parts[0].shape[0]
    sources = gathered(scores, core, edge)
    for d in range(chips):
        for e in range(CORES):
            owner = lax.rem(core + e, CORES)
            block = lax.rem(chip + d, chips) * CORES + owner
            rows = pl.ds(pl.multiple_of(block * edge, edge), edge)
            part = jnp.dot(own[rows, :], sources[0], preferred_element_type=jnp.float32)
            part += jnp.dot(other[rows, :], sources[1], preferred_element_type=jnp.float32)
            if d == 0:
                rows = pl.ds(pl.multiple_of(owner * edge, edge), edge)
                part = damping * part + restart[rows, :]
            ref = parts[d * CORES + e]
            ref[...] = part.astype(ref.dtype)


def final_kernel(chips, *refs):
    parts, out = refs[:-1], refs[-1]
    _, _, core = place()
    topics = parts[0].shape[1]
    for e in range(CORES):
        total = sum(parts[d * CORES + e][...].astype(jnp.float32) for d in range(1, chips))
        lanes = pl.ds(pl.multiple_of(lax.rem(core + e, CORES) * topics, topics), topics)
        out[:, lanes] = parts[e][...] + damping * total


def from_col(value, chips, chip_step, core_step):
    route = [
        (x * CORES + c, (x + chip_step) % chips * CORES + (c + core_step) % CORES)
        for x in range(chips)
        for c in range(CORES)
    ]
    return lax.ppermute(value, "col", route)


def from_blk(value, steps, distance):
    return lax.ppermute(value, "blk", [(i, (i + distance) % steps) for i in range(steps)])


def body(tiles, tile_dest, tile_count, topic_seeds):
    slots, edge = tiles.shape[3], tiles.shape[4]
    steps, columns = lax.axis_size("blk"), lax.axis_size("col")
    chips = columns // CORES
    topics, seeds = topic_seeds.shape[0] // CORES, topic_seeds.shape[1]
    dests, sources, pair = columns * edge, steps * edge, CORES * edge
    groups = -(-steps // PACKED)
    scale = steps * columns * edge / seeds
    f32, bf16, i32 = jnp.float32, jnp.bfloat16, jnp.int32

    def shape(dtype, *dims):
        return jax.ShapeDtypeStruct(dims, dtype)

    def call(kernel, in_specs, outs, room, scratch=()):
        return pl.pallas_call(
            kernel,
            in_specs=in_specs,
            out_shape=outs,
            out_specs=[VMEM] * len(outs),
            scratch_shapes=scratch,
            compiler_params=pltpu.CompilerParams(vmem_limit_bytes=room),
        )

    matrix = 2 * dests * sources
    dense, keep, send, seed_rows = call(
        functools.partial(first_kernel, steps, columns, scale),
        [HBM] * 4,
        [
            shape(bf16, dests, sources),
            shape(f32, dests, topics),
            shape(bf16, dests, topics),
            shape(i32, seeds, topics),
        ],
        6 * MIB + 2 * matrix + 2 * steps * slots * edge * edge,
        [
            pltpu.VMEM((steps, slots, edge, edge), bf16),
            pltpu.SMEM(tile_dest.shape, i32),
            pltpu.SMEM(tile_count.shape, i32),
            pltpu.VMEM((seeds, CORES * topics), i32),
            pltpu.VMEM((dests, edge), f32),
            pltpu.VMEM((CORES, seeds, topics), i32),
            pltpu.VMEM((CORES, groups, seeds, topics), i32),
            pltpu.SemaphoreType.DMA((steps,)),
            pltpu.SemaphoreType.DMA((3,)),
        ],
    )(*(pltpu.with_memory_space_constraint(a, pltpu.HBM) for a in (tiles, tile_dest, tile_count, topic_seeds.T)))
    (restart,) = call(
        functools.partial(restart_kernel, columns, scale),
        [VMEM],
        [shape(f32, pair, topics)],
        4 * MIB,
        [pltpu.VMEM((seeds, topics), i32), pltpu.VMEM((seeds, topics), i32)],
    )(seed_rows)
    recv = from_col(send, chips, 0, 1)
    split = [shape(f32, pair, topics)] + [shape(bf16, pair, topics)] * (chips - 1)
    parts = call(functools.partial(split_kernel, chips), [VMEM] * 2, split, 6 * MIB)(keep, recv)

    other = from_col(dense, chips, 0, 1)
    for iteration in range(ITERS):
        if iteration:
            parts = call(
                functools.partial(step_kernel, chips, steps),
                [VMEM] * (2 + steps),
                split,
                6 * MIB + 2 * matrix,
            )(dense, other, *gather)
        total = parts[0]
        for d in range(1, chips):
            total = total + from_col(parts[d], chips, d, 0).astype(f32)
        sent = (damping * total + restart).astype(bf16)
        gather = [from_blk(sent, steps, d) for d in range(steps - 1, 0, -1)] + [sent]
        if iteration == ITERS - 2:
            break
    parts = call(
        functools.partial(last_kernel, chips, steps),
        [VMEM] * (3 + steps),
        [shape(f32, edge, topics)] * CORES + [shape(bf16, edge, topics)] * (CORES * (chips - 1)),
        6 * MIB + 2 * matrix,
    )(dense, other, restart, *gather)
    arrived = [
        part if d == e == 0 else from_col(part, chips, d, e)
        for (d, e), part in zip([(d, e) for d in range(chips) for e in range(CORES)], parts)
    ]
    (out,) = call(
        functools.partial(final_kernel, chips),
        [VMEM] * len(arrived),
        [shape(f32, edge, CORES * topics)],
        4 * MIB,
    )(*arrived)
    return out


def solution(mesh):
    return jax.shard_map(
        body,
        mesh=mesh,
        in_specs=(
            P(("parts", "blk"), "col", None, None, None, None),
            P(("parts", "blk"), "col", None, None),
            P(("parts", "blk"), "col", None),
            P("parts", None),
        ),
        out_specs=P(("parts", "blk", "col"), None),
        check_vma=False,
    )
```

```python
import functools

import jax
import jax.numpy as jnp
from jax import lax
from jax.experimental import pallas as pl
from jax.experimental.pallas import tpu as pltpu
from jax.sharding import PartitionSpec as P

ITERS = 3
CORES = 2
FIELD = 8
PACKED = 4

damping = 0.85

VMEM = pl.BlockSpec(memory_space=pltpu.VMEM)
HBM = pl.BlockSpec(memory_space=pltpu.HBM)
MIB = 1 << 20


def place():
    col = lax.axis_index("col")
    return lax.axis_index("blk"), col // CORES, col % CORES


def add_seeds(counts, ids, weights, first, last):
    rows = lax.broadcasted_iota(jnp.int32, counts[0].shape, 0)
    for j in range(first, last):
        hit = rows == ids[j : j + 1, :]
        counts = [c + jnp.where(hit, weights[g, j : j + 1, :], 0) for g, c in enumerate(counts)]
    return counts


def field(packed, index):
    return ((packed >> (FIELD * index)) & ((1 << FIELD) - 1)).astype(jnp.float32)


def source_weights(hosts, edge, steps, columns, row, col, weights):
    block = hosts >> (edge.bit_length() - 1)
    step = lax.rem(row - block // columns + steps, steps)
    mine = lax.rem(block, columns) == col
    one = 1 << (FIELD * lax.rem(step, PACKED))
    for g in range(-(-steps // PACKED)):
        weights[g] = jnp.where(mine & (step // PACKED == g), one, 0)
    return block


def source_rows(counts, scale, steps):
    parts = [scale * field(counts[s // PACKED], s % PACKED) for s in range(steps)]
    return jnp.concatenate(parts, axis=0).astype(jnp.bfloat16)


def first_kernel(
    steps, columns, scale, tiles_hbm, dest_hbm, count_hbm, seeds_hbm,
    dense, send, seed_rows,
    tiles, dest, count, seeds, total, ids, weights, tile_sem, table_sem,
):
    slots, edge = tiles.shape[1], tiles.shape[2]
    topics = seeds.shape[1] // CORES
    row, chip, core = place()
    tables = [(seeds_hbm, seeds), (dest_hbm, dest), (count_hbm, count)]
    fetch_tables = [
        pltpu.make_async_copy(source, table, table_sem.at[i]) for i, (source, table) in enumerate(tables)
    ]
    fetch_tiles = [
        pltpu.make_async_copy(tiles_hbm.at[0, 0, s], tiles.at[s], tile_sem.at[s]) for s in range(steps)
    ]
    for fetch in fetch_tables + fetch_tiles:
        fetch.start()

    fetch_tables[0].wait()
    own, other = (
        seeds[:, pl.ds(pl.multiple_of(c * topics, topics), topics)] for c in (core, 1 - core)
    )
    seed_rows[...] = own
    ids[...] = other & (edge - 1)
    source_weights(other, edge, steps, columns, row, chip * CORES + core, weights)
    groups = weights.shape[0]
    counts = [jnp.zeros((edge, topics), jnp.int32)] * groups
    number, done = ids.shape[0], 0

    for fetch in fetch_tables[1:]:
        fetch.wait()
    for s in range(steps):
        upto = number * (steps + 1 + s) // (2 * steps)
        counts = add_seeds(counts, ids, weights, done, upto)
        done = upto
        fetch_tiles[s].wait()
        slot = s % total.shape[0]
        total[slot] = jnp.zeros(total.shape[1:], jnp.float32)
        for t in range(slots):
            block = jnp.where(t < count[0, 0, s], dest[0, 0, s, t], columns)
            rows = pl.ds(pl.multiple_of(block * edge, edge), edge)
            total[slot, rows, :] += tiles[s, t].astype(jnp.float32)
        dense[:, s * edge : (s + 1) * edge] = total[slot, : columns * edge, :].astype(jnp.bfloat16)

    restart = source_rows(counts, scale, steps)
    send[...] = jnp.dot(dense[...], restart, preferred_element_type=jnp.float32).astype(jnp.bfloat16)


def keep_kernel(steps, columns, scale, dense, seed_rows, keep, restart, restart_behind, ids, weights):
    edge = restart.shape[0] // CORES
    row, chip, core = place()
    hosts = seed_rows[...]
    ids[...] = hosts & (edge - 1)
    block = source_weights(hosts, edge, steps, columns, row, chip * CORES + core, weights)
    groups = weights.shape[0] - 1
    weights[groups] = jnp.zeros_like(hosts)
    for d in range(2):
        offset = block - lax.rem(row - d + steps, steps) * columns - chip * CORES
        for c in range(CORES):
            weights[groups] += jnp.where(offset == c, 1 << (FIELD * (d * CORES + c)), 0)
    counts = [jnp.zeros((edge, hosts.shape[1]), jnp.int32)] * (groups + 1)
    counts = add_seeds(counts, ids, weights, 0, ids.shape[0])
    for d, term in enumerate((restart, restart_behind)):
        for c in range(CORES):
            term[c * edge : (c + 1) * edge, :] = (1.0 - damping) * (
                scale * field(counts[groups], d * CORES + c)
            )
    rows = source_rows(counts, scale, steps)
    keep[...] = jnp.dot(dense[...], rows, preferred_element_type=jnp.float32)


def split_kernel(chips, keep, recv, mine, *sends):
    _, chip, _ = place()
    size = mine.shape[0]
    for d in range(chips):
        rows = pl.ds(pl.multiple_of(lax.rem(chip + d, chips) * size, size), size)
        part = keep[rows, :] + recv[rows, :].astype(jnp.float32)
        if d == 0:
            mine[...] = part
        sends[d][...] = part.astype(jnp.bfloat16)


def gathered(scores, core, edge):
    return [
        jnp.concatenate([s[pl.ds(pl.multiple_of(c * edge, edge), edge), :] for s in scores[::-1]], axis=0)
        for c in (core, 1 - core)
    ]


def product(matrices, sources, rows, first):
    lanes = pl.ds(first, sources[0].shape[0])
    return jnp.dot(
        jnp.concatenate([m[rows, lanes] for m in matrices], axis=1),
        jnp.concatenate(sources, axis=0),
        preferred_element_type=jnp.float32,
    )


def near_kernel(own, other, *refs):
    scores, out = refs[:-1], refs[-1]
    _, _, core = place()
    sources = gathered(scores, core, scores[0].shape[0] // CORES)
    out[...] = product((own, other), sources, slice(None), 0)


def step_kernel(chips, first, own, other, near, *refs):
    scores, mine, sends = refs[: -chips - 1], refs[-chips - 1], refs[-chips:]
    _, chip, core = place()
    size = mine.shape[0]
    sources = gathered(scores, core, size // CORES)
    for d in [*range(1, chips), 0]:
        rows = pl.ds(pl.multiple_of(lax.rem(chip + d, chips) * size, size), size)
        part = near[rows, :] + product((own, other), sources, rows, first)
        if d == 0:
            mine[...] = part
        sends[d][...] = part.astype(jnp.bfloat16)


def last_kernel(chips, first, own, other, near, restart, *refs):
    scores, parts = refs[: -chips * CORES], refs[-chips * CORES :]
    _, chip, core = place()
    edge = parts[0].shape[0]
    sources = gathered(scores, core, edge)
    for d in range(chips):
        for e in range(CORES):
            owner = lax.rem(core + e, CORES)
            block = lax.rem(chip + d, chips) * CORES + owner
            rows = pl.ds(pl.multiple_of(block * edge, edge), edge)
            part = near[rows, :] + product((own, other), sources, rows, first)
            if d == 0:
                rows = pl.ds(pl.multiple_of(owner * edge, edge), edge)
                part = damping * part + restart[rows, :]
            ref = parts[d * CORES + e]
            ref[...] = part.astype(ref.dtype)


def final_kernel(chips, *refs):
    parts, out = refs[:-1], refs[-1]
    _, _, core = place()
    topics = parts[0].shape[1]
    for e in range(CORES):
        total = sum(parts[d * CORES + e][...].astype(jnp.float32) for d in range(1, chips))
        lanes = pl.ds(pl.multiple_of(lax.rem(core + e, CORES) * topics, topics), topics)
        out[:, lanes] = parts[e][...] + damping * total


def from_col(value, chips, chip_step, core_step):
    route = [
        (x * CORES + c, (x + chip_step) % chips * CORES + (c + core_step) % CORES)
        for x in range(chips)
        for c in range(CORES)
    ]
    return lax.ppermute(value, "col", route)


def from_behind(value, steps, distance, chips=1, chip_step=0):
    if not chip_step:
        return lax.ppermute(value, "blk", [(i, (i + distance) % steps) for i in range(steps)])
    columns = chips * CORES
    route = [
        (i * columns + x * CORES + c, (i + distance) % steps * columns + (x + chip_step) % chips * CORES + c)
        for i in range(steps)
        for x in range(chips)
        for c in range(CORES)
    ]
    return lax.ppermute(value, ("blk", "col"), route)


def body(tiles, tile_dest, tile_count, topic_seeds):
    slots, edge = tiles.shape[3], tiles.shape[4]
    steps, columns = lax.axis_size("blk"), lax.axis_size("col")
    chips = columns // CORES
    topics, seeds = topic_seeds.shape[0] // CORES, topic_seeds.shape[1]
    dests, sources, pair = columns * edge, steps * edge, CORES * edge
    groups = -(-steps // PACKED)
    scale = steps * columns * edge / seeds
    f32, bf16, i32 = jnp.float32, jnp.bfloat16, jnp.int32

    def shape(dtype, *dims):
        return jax.ShapeDtypeStruct(dims, dtype)

    def call(kernel, in_specs, outs, room, scratch=()):
        return pl.pallas_call(
            kernel,
            in_specs=in_specs,
            out_shape=outs,
            out_specs=[VMEM] * len(outs),
            scratch_shapes=scratch,
            compiler_params=pltpu.CompilerParams(vmem_limit_bytes=room),
        )

    matrix = 2 * dests * sources
    dense, send, seed_rows = call(
        functools.partial(first_kernel, steps, columns, scale),
        [HBM] * 4,
        [shape(bf16, dests, sources), shape(bf16, dests, topics), shape(i32, seeds, topics)],
        6 * MIB + 2 * matrix + 2 * steps * slots * edge * edge,
        [
            pltpu.VMEM((steps, slots, edge, edge), bf16),
            pltpu.SMEM(tile_dest.shape, i32),
            pltpu.SMEM(tile_count.shape, i32),
            pltpu.VMEM((seeds, CORES * topics), i32),
            pltpu.VMEM((2, dests + edge, edge), f32),
            pltpu.VMEM((seeds, topics), i32),
            pltpu.VMEM((groups, seeds, topics), i32),
            pltpu.SemaphoreType.DMA((steps,)),
            pltpu.SemaphoreType.DMA((3,)),
        ],
    )(*(pltpu.with_memory_space_constraint(a, pltpu.HBM) for a in (tiles, tile_dest, tile_count, topic_seeds.T)))
    recv = from_col(send, chips, 0, 1)
    keep, restart, restart_behind = call(
        functools.partial(keep_kernel, steps, columns, scale),
        [VMEM] * 2,
        [shape(f32, dests, topics)] + [shape(f32, pair, topics)] * 2,
        6 * MIB + 2 * matrix,
        [pltpu.VMEM((seeds, topics), i32), pltpu.VMEM((groups + 1, seeds, topics), i32)],
    )(dense, seed_rows)
    split = [shape(f32, pair, topics)] + [shape(bf16, pair, topics)] * chips
    parts = call(functools.partial(split_kernel, chips), [VMEM] * 2, split, 6 * MIB)(keep, recv)

    parts = list(parts)
    parts[0], tied = lax.optimization_barrier((parts[0], dense))
    other = from_col(tied, chips, 0, 1)
    far = steps - 2
    first = 2 * edge
    room = 6 * MIB + 2 * matrix
    for iteration in range(1, ITERS):
        mine, *sends = parts
        total = mine
        for d in range(1, chips):
            total = total + from_col(sends[d], chips, d, 0).astype(f32)
        behind = sum(from_behind(sends[d], steps, 1, chips, d).astype(f32) for d in range(chips))
        sent = (damping * total + restart).astype(bf16)
        sent_behind = (damping * behind + restart_behind).astype(bf16)
        arriving = [from_behind(sent, steps, d) for d in range(steps - 1, 1, -1)]
        (near,) = call(near_kernel, [VMEM] * 4, [shape(f32, dests, topics)], room)(
            dense, other, sent_behind, sent
        )
        if iteration < ITERS - 1:
            parts = call(
                functools.partial(step_kernel, chips, first), [VMEM] * (3 + far), split, room
            )(dense, other, near, *arriving)
        else:
            parts = call(
                functools.partial(last_kernel, chips, first),
                [VMEM] * (4 + far),
                [shape(f32, edge, topics)] * CORES + [shape(bf16, edge, topics)] * (CORES * (chips - 1)),
                room,
            )(dense, other, near, restart, *arriving)
    arrived = [
        part if d == e == 0 else from_col(part, chips, d, e)
        for (d, e), part in zip([(d, e) for d in range(chips) for e in range(CORES)], parts)
    ]
    (out,) = call(
        functools.partial(final_kernel, chips),
        [VMEM] * len(arrived),
        [shape(f32, edge, CORES * topics)],
        4 * MIB,
    )(*arrived)
    return out


def solution(mesh):
    return jax.shard_map(
        body,
        mesh=mesh,
        in_specs=(
            P(("parts", "blk"), "col", None, None, None, None),
            P(("parts", "blk"), "col", None, None),
            P(("parts", "blk"), "col", None),
            P("parts", None),
        ),
        out_specs=P(("parts", "blk", "col"), None),
        check_vma=False,
    )
```

```python
import functools

import jax
import jax.numpy as jnp
from jax import lax
from jax.experimental import pallas as pl
from jax.experimental.pallas import tpu as pltpu
from jax.sharding import PartitionSpec as P

ITERS = 3
CORES = 2
FIELD = 8
PACKED = 4

damping = 0.85

VMEM = pl.BlockSpec(memory_space=pltpu.VMEM)
HBM = pl.BlockSpec(memory_space=pltpu.HBM)
MIB = 1 << 20


def place():
    col = lax.axis_index("col")
    return lax.axis_index("blk"), col // CORES, col % CORES


def cycle(core, steps):
    return list(range(steps)) if core == 0 else [0, *range(1, steps, 2), *range((steps - 1) // 2 * 2, 0, -2)]


def row_behind(row, core, steps, distance):
    place_out = jnp.where(row % 2 == 1, (row + 1) // 2, lax.rem(steps - row // 2, steps))
    at = lax.rem(jnp.where(core == 0, row, place_out) - distance + steps, steps)
    row_out = jnp.where(at <= steps // 2, jnp.maximum(2 * at - 1, 0), 2 * (steps - at))
    return jnp.where(core == 0, at, row_out)


def add_seeds(counts, ids, weights, first, last):
    rows = lax.broadcasted_iota(jnp.int32, counts[0].shape, 0)
    for j in range(first, last):
        hit = rows == ids[j : j + 1, :]
        counts = [c + jnp.where(hit, weights[g, j : j + 1, :], 0) for g, c in enumerate(counts)]
    return counts


def field(packed, index):
    return ((packed >> (FIELD * index)) & ((1 << FIELD) - 1)).astype(jnp.float32)


def source_weights(hosts, edge, steps, columns, row, col, weights):
    block = hosts >> (edge.bit_length() - 1)
    step = lax.rem(row - block // columns + steps, steps)
    mine = lax.rem(block, columns) == col
    one = 1 << (FIELD * lax.rem(step, PACKED))
    for g in range(-(-steps // PACKED)):
        weights[g] = jnp.where(mine & (step // PACKED == g), one, 0)
    return block


def source_rows(counts, scale, steps):
    parts = [scale * field(counts[s // PACKED], s % PACKED) for s in range(steps)]
    return jnp.concatenate(parts, axis=0).astype(jnp.bfloat16)


def first_kernel(
    steps, columns, scale, tiles_hbm, dest_hbm, count_hbm, seeds_hbm,
    dense, send, seed_rows,
    tiles, dest, count, seeds, total, ids, weights, tile_sem, table_sem,
):
    slots, edge = tiles.shape[1], tiles.shape[2]
    topics = seeds.shape[1] // CORES
    row, chip, core = place()
    tables = [(seeds_hbm, seeds), (dest_hbm, dest), (count_hbm, count)]
    fetch_tables = [
        pltpu.make_async_copy(source, table, table_sem.at[i]) for i, (source, table) in enumerate(tables)
    ]
    fetch_tiles = [
        pltpu.make_async_copy(tiles_hbm.at[0, 0, s], tiles.at[s], tile_sem.at[s]) for s in range(steps)
    ]
    for fetch in fetch_tables + fetch_tiles:
        fetch.start()

    fetch_tables[0].wait()
    own, other = (
        seeds[:, pl.ds(pl.multiple_of(c * topics, topics), topics)] for c in (core, 1 - core)
    )
    seed_rows[...] = own
    ids[...] = other & (edge - 1)
    source_weights(other, edge, steps, columns, row, chip * CORES + core, weights)
    groups = weights.shape[0]
    counts = [jnp.zeros((edge, topics), jnp.int32)] * groups
    number, done = ids.shape[0], 0

    for fetch in fetch_tables[1:]:
        fetch.wait()
    for s in range(steps):
        upto = number * (steps + 1 + s) // (2 * steps)
        counts = add_seeds(counts, ids, weights, done, upto)
        done = upto
        fetch_tiles[s].wait()
        slot = s % total.shape[0]
        total[slot] = jnp.zeros(total.shape[1:], jnp.float32)
        for t in range(slots):
            block = jnp.where(t < count[0, 0, s], dest[0, 0, s, t], columns)
            rows = pl.ds(pl.multiple_of(block * edge, edge), edge)
            total[slot, rows, :] += tiles[s, t].astype(jnp.float32)
        dense[:, s * edge : (s + 1) * edge] = total[slot, : columns * edge, :].astype(jnp.bfloat16)

    restart = source_rows(counts, scale, steps)
    send[...] = jnp.dot(dense[...], restart, preferred_element_type=jnp.float32).astype(jnp.bfloat16)


def keep_kernel(steps, columns, scale, dense, seed_rows, keep, restart, restart_behind, ids, weights):
    edge = restart.shape[0] // CORES
    row, chip, core = place()
    hosts = seed_rows[...]
    ids[...] = hosts & (edge - 1)
    block = source_weights(hosts, edge, steps, columns, row, chip * CORES + core, weights)
    groups = weights.shape[0] - 1
    weights[groups] = jnp.zeros_like(hosts)
    for d in range(2):
        offset = block - row_behind(row, core, steps, d) * columns - chip * CORES
        for c in range(CORES):
            weights[groups] += jnp.where(offset == c, 1 << (FIELD * (d * CORES + c)), 0)
    counts = [jnp.zeros((edge, hosts.shape[1]), jnp.int32)] * (groups + 1)
    counts = add_seeds(counts, ids, weights, 0, ids.shape[0])
    for d, term in enumerate((restart, restart_behind)):
        for c in range(CORES):
            term[c * edge : (c + 1) * edge, :] = (1.0 - damping) * (
                scale * field(counts[groups], d * CORES + c)
            )
    rows = source_rows(counts, scale, steps)
    keep[...] = jnp.dot(dense[...], rows, preferred_element_type=jnp.float32)


def split_kernel(chips, keep, recv, mine, *sends):
    _, chip, _ = place()
    size = mine.shape[0]
    for d in range(chips):
        rows = pl.ds(pl.multiple_of(lax.rem(chip + d, chips) * size, size), size)
        part = keep[rows, :] + recv[rows, :].astype(jnp.float32)
        if d == 0:
            mine[...] = part
        sends[d][...] = part.astype(jnp.bfloat16)


def product(matrices, scores, rows, first, steps):
    row, _, core = place()
    edge = scores[0].shape[0] // CORES
    left, right = [], []
    for distance, score in enumerate(scores[::-1], first):
        step = lax.rem(row - row_behind(row, core, steps, distance) + steps, steps)
        for matrix, c in zip(matrices, (core, 1 - core)):
            left.append(matrix[rows, pl.ds(pl.multiple_of(step * edge, edge), edge)])
            right.append(score[pl.ds(pl.multiple_of(c * edge, edge), edge), :])
    return jnp.dot(
        jnp.concatenate(left, axis=1), jnp.concatenate(right, axis=0), preferred_element_type=jnp.float32
    )


def near_kernel(steps, own, other, *refs):
    scores, out = refs[:-1], refs[-1]
    out[...] = product((own, other), scores, slice(None), 0, steps)


def step_kernel(steps, chips, own, other, near, *refs):
    scores, mine, sends = refs[: -chips - 1], refs[-chips - 1], refs[-chips:]
    _, chip, _ = place()
    size = mine.shape[0]
    for d in [*range(1, chips), 0]:
        rows = pl.ds(pl.multiple_of(lax.rem(chip + d, chips) * size, size), size)
        part = near[rows, :] + product((own, other), scores, rows, steps - len(scores), steps)
        if d == 0:
            mine[...] = part
        sends[d][...] = part.astype(jnp.bfloat16)


def last_kernel(steps, chips, own, other, near, restart, *refs):
    scores, parts = refs[: -chips * CORES], refs[-chips * CORES :]
    _, chip, core = place()
    edge = parts[0].shape[0]
    for d in range(chips):
        for e in range(CORES):
            owner = lax.rem(core + e, CORES)
            block = lax.rem(chip + d, chips) * CORES + owner
            rows = pl.ds(pl.multiple_of(block * edge, edge), edge)
            part = near[rows, :] + product((own, other), scores, rows, steps - len(scores), steps)
            if d == 0:
                rows = pl.ds(pl.multiple_of(owner * edge, edge), edge)
                part = damping * part + restart[rows, :]
            ref = parts[d * CORES + e]
            ref[...] = part.astype(ref.dtype)


def final_kernel(chips, *refs):
    parts, out = refs[:-1], refs[-1]
    _, _, core = place()
    topics = parts[0].shape[1]
    for e in range(CORES):
        total = sum(parts[d * CORES + e][...].astype(jnp.float32) for d in range(1, chips))
        lanes = pl.ds(pl.multiple_of(lax.rem(core + e, CORES) * topics, topics), topics)
        out[:, lanes] = parts[e][...] + damping * total


def from_col(value, chips, chip_step, core_step):
    route = [
        (x * CORES + c, (x + chip_step) % chips * CORES + (c + core_step) % CORES)
        for x in range(chips)
        for c in range(CORES)
    ]
    return lax.ppermute(value, "col", route)


def from_behind(value, steps, chips, distance, chip_step=0):
    columns = chips * CORES
    route = []
    for c in range(CORES):
        rows = cycle(c, steps)
        for i in range(steps):
            for x in range(chips):
                target = rows[(i + distance) % steps] * columns + (x + chip_step) % chips * CORES + c
                route.append((rows[i] * columns + x * CORES + c, target))
    return lax.ppermute(value, ("blk", "col"), route)


def body(tiles, tile_dest, tile_count, topic_seeds):
    slots, edge = tiles.shape[3], tiles.shape[4]
    steps, columns = lax.axis_size("blk"), lax.axis_size("col")
    chips = columns // CORES
    topics, seeds = topic_seeds.shape[0] // CORES, topic_seeds.shape[1]
    dests, sources, pair = columns * edge, steps * edge, CORES * edge
    groups = -(-steps // PACKED)
    scale = steps * columns * edge / seeds
    f32, bf16, i32 = jnp.float32, jnp.bfloat16, jnp.int32

    def shape(dtype, *dims):
        return jax.ShapeDtypeStruct(dims, dtype)

    def call(kernel, in_specs, outs, room, scratch=()):
        return pl.pallas_call(
            kernel,
            in_specs=in_specs,
            out_shape=outs,
            out_specs=[VMEM] * len(outs),
            scratch_shapes=scratch,
            compiler_params=pltpu.CompilerParams(vmem_limit_bytes=room),
        )

    matrix = 2 * dests * sources
    dense, send, seed_rows = call(
        functools.partial(first_kernel, steps, columns, scale),
        [HBM] * 4,
        [shape(bf16, dests, sources), shape(bf16, dests, topics), shape(i32, seeds, topics)],
        6 * MIB + 2 * matrix + 2 * steps * slots * edge * edge,
        [
            pltpu.VMEM((steps, slots, edge, edge), bf16),
            pltpu.SMEM(tile_dest.shape, i32),
            pltpu.SMEM(tile_count.shape, i32),
            pltpu.VMEM((seeds, CORES * topics), i32),
            pltpu.VMEM((2, dests + edge, edge), f32),
            pltpu.VMEM((seeds, topics), i32),
            pltpu.VMEM((groups, seeds, topics), i32),
            pltpu.SemaphoreType.DMA((steps,)),
            pltpu.SemaphoreType.DMA((3,)),
        ],
    )(*(pltpu.with_memory_space_constraint(a, pltpu.HBM) for a in (tiles, tile_dest, tile_count, topic_seeds.T)))
    recv = from_col(send, chips, 0, 1)
    keep, restart, restart_behind = call(
        functools.partial(keep_kernel, steps, columns, scale),
        [VMEM] * 2,
        [shape(f32, dests, topics)] + [shape(f32, pair, topics)] * 2,
        6 * MIB + 2 * matrix,
        [pltpu.VMEM((seeds, topics), i32), pltpu.VMEM((groups + 1, seeds, topics), i32)],
    )(dense, seed_rows)
    split = [shape(f32, pair, topics)] + [shape(bf16, pair, topics)] * chips
    parts = call(functools.partial(split_kernel, chips), [VMEM] * 2, split, 6 * MIB)(keep, recv)

    parts = list(parts)
    parts[0], tied = lax.optimization_barrier((parts[0], dense))
    other = from_col(tied, chips, 0, 1)
    far = steps - 2
    room = 6 * MIB + 2 * matrix
    for iteration in range(1, ITERS):
        mine, *sends = parts
        total = mine
        for d in range(1, chips):
            total = total + from_col(sends[d], chips, d, 0).astype(f32)
        behind = sum(from_behind(sends[d], steps, chips, 1, d).astype(f32) for d in range(chips))
        sent = (damping * total + restart).astype(bf16)
        sent_behind = (damping * behind + restart_behind).astype(bf16)
        arriving = [from_behind(sent, steps, chips, d) for d in range(steps - 1, 1, -1)]
        (near,) = call(functools.partial(near_kernel, steps), [VMEM] * 4, [shape(f32, dests, topics)], room)(
            dense, other, sent_behind, sent
        )
        if iteration < ITERS - 1:
            parts = call(
                functools.partial(step_kernel, steps, chips), [VMEM] * (3 + far), split, room
            )(dense, other, near, *arriving)
        else:
            parts = call(
                functools.partial(last_kernel, steps, chips),
                [VMEM] * (4 + far),
                [shape(f32, edge, topics)] * CORES + [shape(bf16, edge, topics)] * (CORES * (chips - 1)),
                room,
            )(dense, other, near, restart, *arriving)
    arrived = [
        part if d == e == 0 else from_col(part, chips, d, e)
        for (d, e), part in zip([(d, e) for d in range(chips) for e in range(CORES)], parts)
    ]
    (out,) = call(
        functools.partial(final_kernel, chips),
        [VMEM] * len(arrived),
        [shape(f32, edge, CORES * topics)],
        4 * MIB,
    )(*arrived)
    return out


def solution(mesh):
    return jax.shard_map(
        body,
        mesh=mesh,
        in_specs=(
            P(("parts", "blk"), "col", None, None, None, None),
            P(("parts", "blk"), "col", None, None),
            P(("parts", "blk"), "col", None),
            P("parts", None),
        ),
        out_specs=P(("parts", "blk", "col"), None),
        check_vma=False,
    )
```

```python
import functools

import jax
import jax.numpy as jnp
from jax import lax
from jax.experimental import pallas as pl
from jax.experimental.pallas import tpu as pltpu
from jax.sharding import PartitionSpec as P

ITERS = 3
CORES = 2
FIELD = 8
PACKED = 4

damping = 0.85

VMEM = pl.BlockSpec(memory_space=pltpu.VMEM)
HBM = pl.BlockSpec(memory_space=pltpu.HBM)
MIB = 1 << 20


def place():
    col = lax.axis_index("col")
    return lax.axis_index("blk"), col // CORES, col % CORES


def cycle(core, steps):
    return list(range(steps)) if core == 0 else [0, *range(1, steps, 2), *range((steps - 1) // 2 * 2, 0, -2)]


def row_behind(row, core, steps, distance):
    place_out = jnp.where(row % 2 == 1, (row + 1) // 2, lax.rem(steps - row // 2, steps))
    at = lax.rem(jnp.where(core == 0, row, place_out) - distance + steps, steps)
    row_out = jnp.where(at <= steps // 2, jnp.maximum(2 * at - 1, 0), 2 * (steps - at))
    return jnp.where(core == 0, at, row_out)


def add_seeds(counts, ids, weights, first, last):
    rows = lax.broadcasted_iota(jnp.int32, counts[0].shape, 0)
    for j in range(first, last):
        hit = rows == ids[j : j + 1, :]
        counts = [c + jnp.where(hit, weights[g, j : j + 1, :], 0) for g, c in enumerate(counts)]
    return counts


def field(packed, index):
    return ((packed >> (FIELD * index)) & ((1 << FIELD) - 1)).astype(jnp.float32)


def source_weights(hosts, edge, steps, columns, row, col, weights):
    block = hosts >> (edge.bit_length() - 1)
    step = lax.rem(row - block // columns + steps, steps)
    mine = lax.rem(block, columns) == col
    one = 1 << (FIELD * lax.rem(step, PACKED))
    for g in range(-(-steps // PACKED)):
        weights[g] = jnp.where(mine & (step // PACKED == g), one, 0)
    return block


def source_rows(counts, scale, steps):
    parts = [scale * field(counts[s // PACKED], s % PACKED) for s in range(steps)]
    return jnp.concatenate(parts, axis=0).astype(jnp.bfloat16)


def first_kernel(
    steps, columns, scale, tiles_hbm, dest_hbm, count_hbm, seeds_hbm,
    dense, send, seed_rows, restart_other,
    tiles, dest, count, seeds, total, ids, weights, tile_sem, table_sem,
):
    slots, edge = tiles.shape[1], tiles.shape[2]
    topics = seeds.shape[1] // CORES
    row, chip, core = place()
    tables = [(seeds_hbm, seeds), (dest_hbm, dest), (count_hbm, count)]
    fetch_tables = [
        pltpu.make_async_copy(source, table, table_sem.at[i]) for i, (source, table) in enumerate(tables)
    ]
    fetch_tiles = [
        pltpu.make_async_copy(tiles_hbm.at[0, 0, s], tiles.at[s], tile_sem.at[s]) for s in range(steps)
    ]
    for fetch in fetch_tables + fetch_tiles:
        fetch.start()

    fetch_tables[0].wait()
    own, other = (
        seeds[:, pl.ds(pl.multiple_of(c * topics, topics), topics)] for c in (core, 1 - core)
    )
    seed_rows[...] = own
    ids[...] = other & (edge - 1)
    source_weights(other, edge, steps, columns, row, chip * CORES + core, weights)
    groups = weights.shape[0]
    counts = [jnp.zeros((edge, topics), jnp.int32)] * groups
    number, done = ids.shape[0], 0

    for fetch in fetch_tables[1:]:
        fetch.wait()
    for s in range(steps):
        upto = number * (steps + 1 + s) // (2 * steps)
        counts = add_seeds(counts, ids, weights, done, upto)
        done = upto
        fetch_tiles[s].wait()
        slot = s % total.shape[0]
        total[slot] = jnp.zeros(total.shape[1:], jnp.float32)
        for t in range(slots):
            block = jnp.where(t < count[0, 0, s], dest[0, 0, s, t], columns)
            rows = pl.ds(pl.multiple_of(block * edge, edge), edge)
            total[slot, rows, :] += tiles[s, t].astype(jnp.float32)
        dense[:, s * edge : (s + 1) * edge] = total[slot, : columns * edge, :].astype(jnp.bfloat16)

    restart_other[...] = (1.0 - damping) * (scale * field(counts[0], 0))
    restart = source_rows(counts, scale, steps)
    send[...] = jnp.dot(dense[...], restart, preferred_element_type=jnp.float32).astype(jnp.bfloat16)


def keep_kernel(steps, columns, scale, dense, seed_rows, keep, restart, restart_behind, ids, weights):
    edge = restart.shape[0] // CORES
    row, chip, core = place()
    hosts = seed_rows[...]
    ids[...] = hosts & (edge - 1)
    block = source_weights(hosts, edge, steps, columns, row, chip * CORES + core, weights)
    groups = weights.shape[0] - 1
    weights[groups] = jnp.zeros_like(hosts)
    for d in range(2):
        offset = block - row_behind(row, core, steps, d) * columns - chip * CORES
        for c in range(CORES):
            weights[groups] += jnp.where(offset == c, 1 << (FIELD * (d * CORES + c)), 0)
    counts = [jnp.zeros((edge, hosts.shape[1]), jnp.int32)] * (groups + 1)
    counts = add_seeds(counts, ids, weights, 0, ids.shape[0])
    for d, term in enumerate((restart, restart_behind)):
        for c in range(CORES):
            term[c * edge : (c + 1) * edge, :] = (1.0 - damping) * (
                scale * field(counts[groups], d * CORES + c)
            )
    rows = source_rows(counts, scale, steps)
    keep[...] = jnp.dot(dense[...], rows, preferred_element_type=jnp.float32)


def split_kernel(chips, keep, recv, mine, *sends):
    _, chip, _ = place()
    size = mine.shape[0]
    for d in range(chips):
        rows = pl.ds(pl.multiple_of(lax.rem(chip + d, chips) * size, size), size)
        part = keep[rows, :] + recv[rows, :].astype(jnp.float32)
        if d == 0:
            mine[...] = part
        sends[d][...] = part.astype(jnp.bfloat16)


def product(matrices, scores, rows, first, steps):
    row, _, core = place()
    edge = scores[0].shape[0] // CORES
    left, right = [], []
    for distance, score in enumerate(scores[::-1], first):
        step = lax.rem(row - row_behind(row, core, steps, distance) + steps, steps)
        for matrix, c in zip(matrices, (core, 1 - core)):
            left.append(matrix[rows, pl.ds(pl.multiple_of(step * edge, edge), edge)])
            right.append(score[pl.ds(pl.multiple_of(c * edge, edge), edge), :])
    return jnp.dot(
        jnp.concatenate(left, axis=1), jnp.concatenate(right, axis=0), preferred_element_type=jnp.float32
    )


def near_kernel(steps, own, other, *refs):
    scores, out = refs[:-1], refs[-1]
    out[...] = product((own, other), scores, slice(None), 0, steps)


def step_kernel(steps, chips, own, other, near, *refs):
    scores, mine, sends = refs[: -chips - 1], refs[-chips - 1], refs[-chips:]
    _, chip, _ = place()
    size = mine.shape[0]
    for d in [*range(1, chips), 0]:
        rows = pl.ds(pl.multiple_of(lax.rem(chip + d, chips) * size, size), size)
        part = near[rows, :] + product((own, other), scores, rows, steps - len(scores), steps)
        if d == 0:
            mine[...] = part
        sends[d][...] = part.astype(jnp.bfloat16)


def last_kernel(steps, chips, own, other, near, restart, *refs):
    scores, parts = refs[: -chips * CORES], refs[-chips * CORES :]
    _, chip, core = place()
    edge = parts[0].shape[0]
    for d in range(chips):
        for e in range(CORES):
            owner = lax.rem(core + e, CORES)
            block = lax.rem(chip + d, chips) * CORES + owner
            rows = pl.ds(pl.multiple_of(block * edge, edge), edge)
            part = near[rows, :] + product((own, other), scores, rows, steps - len(scores), steps)
            if d == e == 0:
                rows = pl.ds(pl.multiple_of(core * edge, edge), edge)
                part = damping * part + restart[rows, :]
            ref = parts[d * CORES + e]
            ref[...] = part.astype(ref.dtype)


def final_kernel(chips, own, restart, *refs):
    parts, out = refs[:-1], refs[-1]
    _, _, core = place()
    topics = own.shape[1]
    for e in range(CORES):
        total = sum(ref[...].astype(jnp.float32) for ref in parts[e::CORES])
        lanes = pl.ds(pl.multiple_of(lax.rem(core + 1 - e, CORES) * topics, topics), topics)
        out[:, lanes] = (restart if e == 0 else own)[...] + damping * total


def from_col(value, chips, chip_step, core_step):
    route = [
        (x * CORES + c, (x + chip_step) % chips * CORES + (c + core_step) % CORES)
        for x in range(chips)
        for c in range(CORES)
    ]
    return lax.ppermute(value, "col", route)


def from_behind(value, steps, chips, distance, chip_step=0):
    columns = chips * CORES
    route = []
    for c in range(CORES):
        rows = cycle(c, steps)
        for i in range(steps):
            for x in range(chips):
                target = rows[(i + distance) % steps] * columns + (x + chip_step) % chips * CORES + c
                route.append((rows[i] * columns + x * CORES + c, target))
    return lax.ppermute(value, ("blk", "col"), route)


def body(tiles, tile_dest, tile_count, topic_seeds):
    slots, edge = tiles.shape[3], tiles.shape[4]
    steps, columns = lax.axis_size("blk"), lax.axis_size("col")
    chips = columns // CORES
    topics, seeds = topic_seeds.shape[0] // CORES, topic_seeds.shape[1]
    dests, sources, pair = columns * edge, steps * edge, CORES * edge
    groups = -(-steps // PACKED)
    scale = steps * columns * edge / seeds
    f32, bf16, i32 = jnp.float32, jnp.bfloat16, jnp.int32

    def shape(dtype, *dims):
        return jax.ShapeDtypeStruct(dims, dtype)

    def call(kernel, in_specs, outs, room, scratch=()):
        return pl.pallas_call(
            kernel,
            in_specs=in_specs,
            out_shape=outs,
            out_specs=[VMEM] * len(outs),
            scratch_shapes=scratch,
            compiler_params=pltpu.CompilerParams(vmem_limit_bytes=room),
        )

    matrix = 2 * dests * sources
    dense, send, seed_rows, restart_other = call(
        functools.partial(first_kernel, steps, columns, scale),
        [HBM] * 4,
        [
            shape(bf16, dests, sources),
            shape(bf16, dests, topics),
            shape(i32, seeds, topics),
            shape(f32, edge, topics),
        ],
        6 * MIB + 2 * matrix + 2 * steps * slots * edge * edge,
        [
            pltpu.VMEM((steps, slots, edge, edge), bf16),
            pltpu.SMEM(tile_dest.shape, i32),
            pltpu.SMEM(tile_count.shape, i32),
            pltpu.VMEM((seeds, CORES * topics), i32),
            pltpu.VMEM((2, dests + edge, edge), f32),
            pltpu.VMEM((seeds, topics), i32),
            pltpu.VMEM((groups, seeds, topics), i32),
            pltpu.SemaphoreType.DMA((steps,)),
            pltpu.SemaphoreType.DMA((3,)),
        ],
    )(*(pltpu.with_memory_space_constraint(a, pltpu.HBM) for a in (tiles, tile_dest, tile_count, topic_seeds.T)))
    recv = from_col(send, chips, 0, 1)
    keep, restart, restart_behind = call(
        functools.partial(keep_kernel, steps, columns, scale),
        [VMEM] * 2,
        [shape(f32, dests, topics)] + [shape(f32, pair, topics)] * 2,
        6 * MIB + 2 * matrix,
        [pltpu.VMEM((seeds, topics), i32), pltpu.VMEM((groups + 1, seeds, topics), i32)],
    )(dense, seed_rows)
    split = [shape(f32, pair, topics)] + [shape(bf16, pair, topics)] * chips
    parts = call(functools.partial(split_kernel, chips), [VMEM] * 2, split, 6 * MIB)(keep, recv)

    parts = list(parts)
    parts[0], tied = lax.optimization_barrier((parts[0], dense))
    other = from_col(tied, chips, 0, 1)
    far = steps - 2
    room = 6 * MIB + 2 * matrix
    for iteration in range(1, ITERS):
        mine, *sends = parts
        total = mine
        for d in range(1, chips):
            total = total + from_col(sends[d], chips, d, 0).astype(f32)
        behind = sum(from_behind(sends[d], steps, chips, 1, d).astype(f32) for d in range(chips))
        sent = (damping * total + restart).astype(bf16)
        sent_behind = (damping * behind + restart_behind).astype(bf16)
        arriving = [from_behind(sent, steps, chips, d) for d in range(steps - 1, 1, -1)]
        (near,) = call(functools.partial(near_kernel, steps), [VMEM] * 4, [shape(f32, dests, topics)], room)(
            dense, other, sent_behind, sent
        )
        if iteration < ITERS - 1:
            parts = call(
                functools.partial(step_kernel, steps, chips), [VMEM] * (3 + far), split, room
            )(dense, other, near, *arriving)
        else:
            parts = call(
                functools.partial(last_kernel, steps, chips),
                [VMEM] * (4 + far),
                [shape(f32, edge, topics)] + [shape(bf16, edge, topics)] * (CORES * chips - 1),
                room,
            )(dense, other, near, restart, *arriving)
    own, core, *away = parts
    moved = [from_col(core, chips, 0, 1)]
    moved += [from_col(part, chips, 1 + i // CORES, i % CORES) for i, part in enumerate(away)]
    (out,) = call(
        functools.partial(final_kernel, chips),
        [VMEM] * (2 + len(moved)),
        [shape(f32, edge, CORES * topics)],
        4 * MIB,
    )(own, restart_other, *moved[:0:-1], moved[0])
    return out


def solution(mesh):
    return jax.shard_map(
        body,
        mesh=mesh,
        in_specs=(
            P(("parts", "blk"), "col", None, None, None, None),
            P(("parts", "blk"), "col", None, None),
            P(("parts", "blk"), "col", None),
            P("parts", None),
        ),
        out_specs=P(("parts", "blk", "col"), None),
        check_vma=False,
    )
```

```python
import functools

import jax
import jax.numpy as jnp
from jax import lax
from jax.experimental import pallas as pl
from jax.experimental.pallas import tpu as pltpu
from jax.sharding import PartitionSpec as P

ITERS = 3
CORES = 2
FIELD = 8
PACKED = 4
LOW = 32

damping = 0.85

VMEM = pl.BlockSpec(memory_space=pltpu.VMEM)
HBM = pl.BlockSpec(memory_space=pltpu.HBM)
MIB = 1 << 20


def place():
    col = lax.axis_index("col")
    return lax.axis_index("blk"), col // CORES, col % CORES


def cycle(core, steps):
    return list(range(steps)) if core == 0 else [0, *range(1, steps, 2), *range((steps - 1) // 2 * 2, 0, -2)]


def row_behind(row, core, steps, distance):
    place_out = jnp.where(row % 2 == 1, (row + 1) // 2, lax.rem(steps - row // 2, steps))
    at = lax.rem(jnp.where(core == 0, row, place_out) - distance + steps, steps)
    row_out = jnp.where(at <= steps // 2, jnp.maximum(2 * at - 1, 0), 2 * (steps - at))
    return jnp.where(core == 0, at, row_out)


def add_seeds(counts, ids, weights, first, last):
    rows = lax.broadcasted_iota(jnp.int32, counts[0].shape, 0)
    for j in range(first, last):
        hit = rows == ids[j : j + 1, :]
        counts = [c + jnp.where(hit, weights[g, j : j + 1, :], 0) for g, c in enumerate(counts)]
    return counts


def field(packed, index):
    return ((packed >> (FIELD * index)) & ((1 << FIELD) - 1)).astype(jnp.float32)


def source_weights(hosts, edge, steps, columns, row, col, weights):
    block = hosts >> (edge.bit_length() - 1)
    step = lax.rem(row - block // columns + steps, steps)
    mine = lax.rem(block, columns) == col
    one = 1 << (FIELD * lax.rem(step, PACKED))
    for g in range(-(-steps // PACKED)):
        weights[g] = jnp.where(mine & (step // PACKED == g), one, 0)
    return block


def source_rows(counts, scale, steps):
    parts = [scale * field(counts[s // PACKED], s % PACKED) for s in range(steps)]
    return jnp.concatenate(parts, axis=0).astype(jnp.bfloat16)


def first_kernel(
    steps, columns, scale, tiles_hbm, dest_hbm, count_hbm, seeds_hbm,
    dense, send, seed_rows, restart_other,
    tiles, dest, count, seeds, total, ids, weights, split, tile_sem, table_sem,
):
    slots, edge = tiles.shape[1], tiles.shape[2]
    topics = seeds.shape[1] // CORES
    row, chip, core = place()
    tables = [(seeds_hbm, seeds), (dest_hbm, dest), (count_hbm, count)]
    fetch_tables = [
        pltpu.make_async_copy(source, table, table_sem.at[i]) for i, (source, table) in enumerate(tables)
    ]
    fetch_tiles = [
        pltpu.make_async_copy(tiles_hbm.at[0, 0, s], tiles.at[s], tile_sem.at[s]) for s in range(steps)
    ]
    for fetch in fetch_tables + fetch_tiles:
        fetch.start()

    fetch_tables[0].wait()
    own, other = (
        seeds[:, pl.ds(pl.multiple_of(c * topics, topics), topics)] for c in (core, 1 - core)
    )
    seed_rows[...] = own
    ids[...] = other & (LOW - 1)
    source_weights(other, edge, steps, columns, row, chip * CORES + core, weights)
    high = (other & (edge - 1)) // LOW
    parts = edge // LOW
    for g in range(weights.shape[0]):
        for h in range(parts):
            split[g * parts + h] = jnp.where(high == h, weights[g], 0)
    counts = [jnp.zeros((LOW, topics), jnp.int32)] * split.shape[0]
    number, done = ids.shape[0], 0

    for fetch in fetch_tables[1:]:
        fetch.wait()
    for s in range(steps):
        upto = number * (steps + 1 + s) // (2 * steps)
        counts = add_seeds(counts, ids, split, done, upto)
        done = upto
        fetch_tiles[s].wait()
        slot = s % total.shape[0]
        total[slot] = jnp.zeros(total.shape[1:], jnp.float32)
        for t in range(slots):
            block = jnp.where(t < count[0, 0, s], dest[0, 0, s, t], columns)
            rows = pl.ds(pl.multiple_of(block * edge, edge), edge)
            total[slot, rows, :] += tiles[s, t].astype(jnp.float32)
        dense[:, s * edge : (s + 1) * edge] = total[slot, : columns * edge, :].astype(jnp.bfloat16)

    counts = [jnp.concatenate(counts[g : g + parts], axis=0) for g in range(0, len(counts), parts)]
    restart_other[...] = (1.0 - damping) * (scale * field(counts[0], 0))
    restart = source_rows(counts, scale, steps)
    send[...] = jnp.dot(dense[...], restart, preferred_element_type=jnp.float32).astype(jnp.bfloat16)


def keep_kernel(steps, columns, scale, dense, seed_rows, keep, restart, restart_behind, ids, weights):
    edge = restart.shape[0] // CORES
    row, chip, core = place()
    hosts = seed_rows[...]
    ids[...] = hosts & (edge - 1)
    block = source_weights(hosts, edge, steps, columns, row, chip * CORES + core, weights)
    groups = weights.shape[0] - 1
    weights[groups] = jnp.zeros_like(hosts)
    for d in range(2):
        offset = block - row_behind(row, core, steps, d) * columns - chip * CORES
        for c in range(CORES):
            weights[groups] += jnp.where(offset == c, 1 << (FIELD * (d * CORES + c)), 0)
    counts = [jnp.zeros((edge, hosts.shape[1]), jnp.int32)] * (groups + 1)
    counts = add_seeds(counts, ids, weights, 0, ids.shape[0])
    for d, term in enumerate((restart, restart_behind)):
        for c in range(CORES):
            term[c * edge : (c + 1) * edge, :] = (1.0 - damping) * (
                scale * field(counts[groups], d * CORES + c)
            )
    rows = source_rows(counts, scale, steps)
    keep[...] = jnp.dot(dense[...], rows, preferred_element_type=jnp.float32)


def split_kernel(chips, keep, recv, mine, *sends):
    _, chip, _ = place()
    size = mine.shape[0]
    for d in range(chips):
        rows = pl.ds(pl.multiple_of(lax.rem(chip + d, chips) * size, size), size)
        part = keep[rows, :] + recv[rows, :].astype(jnp.float32)
        if d == 0:
            mine[...] = part
        sends[d][...] = part.astype(jnp.bfloat16)


def product(matrices, scores, rows, first, steps):
    row, _, core = place()
    edge = scores[0].shape[0] // CORES
    left, right = [], []
    for distance, score in enumerate(scores[::-1], first):
        step = lax.rem(row - row_behind(row, core, steps, distance) + steps, steps)
        for matrix, c in zip(matrices, (core, 1 - core)):
            left.append(matrix[rows, pl.ds(pl.multiple_of(step * edge, edge), edge)])
            right.append(score[pl.ds(pl.multiple_of(c * edge, edge), edge), :])
    return jnp.dot(
        jnp.concatenate(left, axis=1), jnp.concatenate(right, axis=0), preferred_element_type=jnp.float32
    )


def near_kernel(steps, own, other, *refs):
    scores, out = refs[:-1], refs[-1]
    out[...] = product((own, other), scores, slice(None), 0, steps)


def step_kernel(steps, chips, own, other, near, *refs):
    scores, mine, sends = refs[: -chips - 1], refs[-chips - 1], refs[-chips:]
    _, chip, _ = place()
    size = mine.shape[0]
    for d in [*range(1, chips), 0]:
        rows = pl.ds(pl.multiple_of(lax.rem(chip + d, chips) * size, size), size)
        part = near[rows, :] + product((own, other), scores, rows, steps - len(scores), steps)
        if d == 0:
            mine[...] = part
        sends[d][...] = part.astype(jnp.bfloat16)


def last_kernel(steps, chips, first, own, other, near, restart, *refs):
    scores, parts = refs[: steps - 2], refs[steps - 2 :]
    _, chip, core = place()
    edge = parts[0].shape[0]
    for i, ref in enumerate(parts):
        d, e = first + i // CORES, i % CORES
        block = lax.rem(chip + d, chips) * CORES + lax.rem(core + e, CORES)
        rows = pl.ds(pl.multiple_of(block * edge, edge), edge)
        part = near[rows, :] + product((own, other), scores, rows, steps - len(scores), steps)
        if d == e == 0:
            rows = pl.ds(pl.multiple_of(core * edge, edge), edge)
            part = damping * part + restart[rows, :]
        ref[...] = part.astype(ref.dtype)


def final_kernel(chips, own, restart, *refs):
    parts, out = refs[:-1], refs[-1]
    _, _, core = place()
    topics = own.shape[1]
    for e in range(CORES):
        total = sum(ref[...].astype(jnp.float32) for ref in parts[e::CORES])
        lanes = pl.ds(pl.multiple_of(lax.rem(core + 1 - e, CORES) * topics, topics), topics)
        out[:, lanes] = (restart if e == 0 else own)[...] + damping * total


def from_col(value, chips, chip_step, core_step):
    route = [
        (x * CORES + c, (x + chip_step) % chips * CORES + (c + core_step) % CORES)
        for x in range(chips)
        for c in range(CORES)
    ]
    return lax.ppermute(value, "col", route)


def from_behind(value, steps, chips, distance, chip_step=0):
    columns = chips * CORES
    route = []
    for c in range(CORES):
        rows = cycle(c, steps)
        for i in range(steps):
            for x in range(chips):
                target = rows[(i + distance) % steps] * columns + (x + chip_step) % chips * CORES + c
                route.append((rows[i] * columns + x * CORES + c, target))
    return lax.ppermute(value, ("blk", "col"), route)


def body(tiles, tile_dest, tile_count, topic_seeds):
    slots, edge = tiles.shape[3], tiles.shape[4]
    steps, columns = lax.axis_size("blk"), lax.axis_size("col")
    chips = columns // CORES
    topics, seeds = topic_seeds.shape[0] // CORES, topic_seeds.shape[1]
    dests, sources, pair = columns * edge, steps * edge, CORES * edge
    groups = -(-steps // PACKED)
    scale = steps * columns * edge / seeds
    f32, bf16, i32 = jnp.float32, jnp.bfloat16, jnp.int32

    def shape(dtype, *dims):
        return jax.ShapeDtypeStruct(dims, dtype)

    def call(kernel, in_specs, outs, room, scratch=()):
        return pl.pallas_call(
            kernel,
            in_specs=in_specs,
            out_shape=outs,
            out_specs=[VMEM] * len(outs),
            scratch_shapes=scratch,
            compiler_params=pltpu.CompilerParams(vmem_limit_bytes=room),
        )

    matrix = 2 * dests * sources
    dense, send, seed_rows, restart_other = call(
        functools.partial(first_kernel, steps, columns, scale),
        [HBM] * 4,
        [
            shape(bf16, dests, sources),
            shape(bf16, dests, topics),
            shape(i32, seeds, topics),
            shape(f32, edge, topics),
        ],
        6 * MIB + 2 * matrix + 2 * steps * slots * edge * edge,
        [
            pltpu.VMEM((steps, slots, edge, edge), bf16),
            pltpu.SMEM(tile_dest.shape, i32),
            pltpu.SMEM(tile_count.shape, i32),
            pltpu.VMEM((seeds, CORES * topics), i32),
            pltpu.VMEM((2, dests + edge, edge), f32),
            pltpu.VMEM((seeds, topics), i32),
            pltpu.VMEM((groups, seeds, topics), i32),
            pltpu.VMEM((groups * edge // LOW, seeds, topics), i32),
            pltpu.SemaphoreType.DMA((steps,)),
            pltpu.SemaphoreType.DMA((3,)),
        ],
    )(*(pltpu.with_memory_space_constraint(a, pltpu.HBM) for a in (tiles, tile_dest, tile_count, topic_seeds.T)))
    recv = from_col(send, chips, 0, 1)
    keep, restart, restart_behind = call(
        functools.partial(keep_kernel, steps, columns, scale),
        [VMEM] * 2,
        [shape(f32, dests, topics)] + [shape(f32, pair, topics)] * 2,
        6 * MIB + 2 * matrix,
        [pltpu.VMEM((seeds, topics), i32), pltpu.VMEM((groups + 1, seeds, topics), i32)],
    )(dense, seed_rows)
    split = [shape(f32, pair, topics)] + [shape(bf16, pair, topics)] * chips
    parts = call(functools.partial(split_kernel, chips), [VMEM] * 2, split, 6 * MIB)(keep, recv)

    parts = list(parts)
    parts[0], tied = lax.optimization_barrier((parts[0], dense))
    other = from_col(tied, chips, 0, 1)
    far = steps - 2
    room = 6 * MIB + 2 * matrix
    for iteration in range(1, ITERS):
        mine, *sends = parts
        total = mine
        for d in range(1, chips):
            total = total + from_col(sends[d], chips, d, 0).astype(f32)
        behind = sum(from_behind(sends[d], steps, chips, 1, d).astype(f32) for d in range(chips))
        sent = (damping * total + restart).astype(bf16)
        sent_behind = (damping * behind + restart_behind).astype(bf16)
        arriving = [from_behind(sent, steps, chips, d) for d in range(steps - 1, 1, -1)]
        (near,) = call(functools.partial(near_kernel, steps), [VMEM] * 4, [shape(f32, dests, topics)], room)(
            dense, other, sent_behind, sent
        )
        if iteration < ITERS - 1:
            parts = call(
                functools.partial(step_kernel, steps, chips), [VMEM] * (3 + far), split, room
            )(dense, other, near, *arriving)
        else:
            away = call(
                functools.partial(last_kernel, steps, chips, 1),
                [VMEM] * (4 + far),
                [shape(bf16, edge, topics)] * (CORES * (chips - 1)),
                room,
            )(dense, other, near, restart, *arriving)
            home = call(
                functools.partial(last_kernel, steps, chips, 0),
                [VMEM] * (4 + far),
                [shape(f32, edge, topics), shape(bf16, edge, topics)],
                room,
            )(dense, other, near, restart, *arriving)
            parts = [*home, *away]
    own, core, *away = parts
    moved = [from_col(core, chips, 0, 1)]
    moved += [from_col(part, chips, 1 + i // CORES, i % CORES) for i, part in enumerate(away)]
    (out,) = call(
        functools.partial(final_kernel, chips),
        [VMEM] * (2 + len(moved)),
        [shape(f32, edge, CORES * topics)],
        4 * MIB,
    )(own, restart_other, *moved[:0:-1], moved[0])
    return out


def solution(mesh):
    return jax.shard_map(
        body,
        mesh=mesh,
        in_specs=(
            P(("parts", "blk"), "col", None, None, None, None),
            P(("parts", "blk"), "col", None, None),
            P(("parts", "blk"), "col", None),
            P("parts", None),
        ),
        out_specs=P(("parts", "blk", "col"), None),
        check_vma=False,
    )
```

```python
import functools

import jax
import jax.numpy as jnp
from jax import lax
from jax.experimental import pallas as pl
from jax.experimental.pallas import tpu as pltpu
from jax.sharding import PartitionSpec as P

ITERS = 3
CORES = 2
FIELD = 8
PACKED = 4
LOW = 32

damping = 0.85

VMEM = pl.BlockSpec(memory_space=pltpu.VMEM)
HBM = pl.BlockSpec(memory_space=pltpu.HBM)
MIB = 1 << 20


def place():
    col = lax.axis_index("col")
    return lax.axis_index("blk"), col // CORES, col % CORES


def cycle(core, steps):
    return list(range(steps)) if core == 0 else [0, *range(1, steps, 2), *range((steps - 1) // 2 * 2, 0, -2)]


def row_behind(row, core, steps, distance):
    place_out = jnp.where(row % 2 == 1, (row + 1) // 2, lax.rem(steps - row // 2, steps))
    at = lax.rem(jnp.where(core == 0, row, place_out) - distance + steps, steps)
    row_out = jnp.where(at <= steps // 2, jnp.maximum(2 * at - 1, 0), 2 * (steps - at))
    return jnp.where(core == 0, at, row_out)


def add_seeds(counts, ids, weights, first, last):
    rows = lax.broadcasted_iota(jnp.int32, counts[0].shape, 0)
    for j in range(first, last):
        hit = rows == ids[j : j + 1, :]
        counts = [c + jnp.where(hit, weights[g, j : j + 1, :], 0) for g, c in enumerate(counts)]
    return counts


def field(packed, index):
    return ((packed >> (FIELD * index)) & ((1 << FIELD) - 1)).astype(jnp.float32)


def source_weights(hosts, edge, steps, columns, row, col, weights):
    block = hosts >> (edge.bit_length() - 1)
    step = lax.rem(row - block // columns + steps, steps)
    mine = lax.rem(block, columns) == col
    one = 1 << (FIELD * lax.rem(step, PACKED))
    for g in range(-(-steps // PACKED)):
        weights[g] = jnp.where(mine & (step // PACKED == g), one, 0)
    return block


def source_rows(counts, scale, steps):
    parts = [scale * field(counts[s // PACKED], s % PACKED) for s in range(steps)]
    return jnp.concatenate(parts, axis=0).astype(jnp.bfloat16)


def first_kernel(
    steps, columns, scale, tiles_hbm, dest_hbm, count_hbm, seeds_hbm,
    dense, send, seed_rows, restart_other,
    tiles, dest, count, seeds, total, ids, weights, split, tile_sem, table_sem,
):
    slots, edge = tiles.shape[1], tiles.shape[2]
    topics = seeds.shape[1] // CORES
    row, chip, core = place()
    tables = [(seeds_hbm, seeds), (dest_hbm, dest), (count_hbm, count)]
    fetch_tables = [
        pltpu.make_async_copy(source, table, table_sem.at[i]) for i, (source, table) in enumerate(tables)
    ]
    fetch_tiles = [
        pltpu.make_async_copy(tiles_hbm.at[0, 0, s], tiles.at[s], tile_sem.at[s]) for s in range(steps)
    ]
    for fetch in fetch_tables + fetch_tiles:
        fetch.start()

    fetch_tables[0].wait()
    own, other = (
        seeds[:, pl.ds(pl.multiple_of(c * topics, topics), topics)] for c in (core, 1 - core)
    )
    seed_rows[...] = own
    ids[...] = other & (LOW - 1)
    source_weights(other, edge, steps, columns, row, chip * CORES + core, weights)
    high = (other & (edge - 1)) // LOW
    parts = edge // LOW
    for g in range(weights.shape[0]):
        for h in range(parts):
            split[g * parts + h] = jnp.where(high == h, weights[g], 0)
    counts = [jnp.zeros((LOW, topics), jnp.int32)] * split.shape[0]
    number, done = ids.shape[0], 0

    for fetch in fetch_tables[1:]:
        fetch.wait()
    for s in range(steps):
        upto = number * (s + 1) // steps
        counts = add_seeds(counts, ids, split, done, upto)
        done = upto
        fetch_tiles[s].wait()
        slot = s % total.shape[0]
        total[slot] = jnp.zeros(total.shape[1:], jnp.float32)
        for t in range(slots):
            block = jnp.where(t < count[0, 0, s], dest[0, 0, s, t], columns)
            rows = pl.ds(pl.multiple_of(block * edge, edge), edge)
            total[slot, rows, :] += tiles[s, t].astype(jnp.float32)
        dense[:, s * edge : (s + 1) * edge] = total[slot, : columns * edge, :].astype(jnp.bfloat16)

    counts = [jnp.concatenate(counts[g : g + parts], axis=0) for g in range(0, len(counts), parts)]
    restart_other[...] = (1.0 - damping) * (scale * field(counts[0], 0))
    restart = source_rows(counts, scale, steps)
    send[...] = jnp.dot(dense[...], restart, preferred_element_type=jnp.float32).astype(jnp.bfloat16)


def keep_kernel(steps, columns, scale, dense, seed_rows, keep, restart, restart_behind, ids, weights):
    edge = restart.shape[0] // CORES
    row, chip, core = place()
    hosts = seed_rows[...]
    ids[...] = hosts & (edge - 1)
    block = source_weights(hosts, edge, steps, columns, row, chip * CORES + core, weights)
    groups = weights.shape[0] - 1
    weights[groups] = jnp.zeros_like(hosts)
    for d in range(2):
        offset = block - row_behind(row, core, steps, d) * columns - chip * CORES
        for c in range(CORES):
            weights[groups] += jnp.where(offset == c, 1 << (FIELD * (d * CORES + c)), 0)
    counts = [jnp.zeros((edge, hosts.shape[1]), jnp.int32)] * (groups + 1)
    counts = add_seeds(counts, ids, weights, 0, ids.shape[0])
    for d, term in enumerate((restart, restart_behind)):
        for c in range(CORES):
            term[c * edge : (c + 1) * edge, :] = (1.0 - damping) * (
                scale * field(counts[groups], d * CORES + c)
            )
    rows = source_rows(counts, scale, steps)
    keep[...] = jnp.dot(dense[...], rows, preferred_element_type=jnp.float32)


def split_kernel(chips, keep, recv, mine, *sends):
    _, chip, _ = place()
    size = mine.shape[0]
    for d in range(chips):
        rows = pl.ds(pl.multiple_of(lax.rem(chip + d, chips) * size, size), size)
        part = keep[rows, :] + recv[rows, :].astype(jnp.float32)
        if d == 0:
            mine[...] = part
        sends[d][...] = part.astype(jnp.bfloat16)


def product(matrices, scores, rows, first, steps):
    row, _, core = place()
    edge = scores[0].shape[0] // CORES
    left, right = [], []
    for distance, score in enumerate(scores[::-1], first):
        step = lax.rem(row - row_behind(row, core, steps, distance) + steps, steps)
        for matrix, c in zip(matrices, (core, 1 - core)):
            left.append(matrix[rows, pl.ds(pl.multiple_of(step * edge, edge), edge)])
            right.append(score[pl.ds(pl.multiple_of(c * edge, edge), edge), :])
    return jnp.dot(
        jnp.concatenate(left, axis=1), jnp.concatenate(right, axis=0), preferred_element_type=jnp.float32
    )


def near_kernel(steps, own, other, *refs):
    scores, out = refs[:-1], refs[-1]
    out[...] = product((own, other), scores, slice(None), 0, steps)


def step_kernel(steps, chips, own, other, near, *refs):
    scores, mine, sends = refs[: -chips - 1], refs[-chips - 1], refs[-chips:]
    _, chip, _ = place()
    size = mine.shape[0]
    for d in [*range(1, chips), 0]:
        rows = pl.ds(pl.multiple_of(lax.rem(chip + d, chips) * size, size), size)
        part = near[rows, :] + product((own, other), scores, rows, steps - len(scores), steps)
        if d == 0:
            mine[...] = part
        sends[d][...] = part.astype(jnp.bfloat16)


def last_kernel(steps, chips, first, own, other, near, restart, *refs):
    scores, parts = refs[: steps - 2], refs[steps - 2 :]
    _, chip, core = place()
    edge = parts[0].shape[0]
    for i, ref in enumerate(parts):
        d, e = first + i // CORES, i % CORES
        block = lax.rem(chip + d, chips) * CORES + lax.rem(core + e, CORES)
        rows = pl.ds(pl.multiple_of(block * edge, edge), edge)
        part = near[rows, :] + product((own, other), scores, rows, steps - len(scores), steps)
        if d == e == 0:
            rows = pl.ds(pl.multiple_of(core * edge, edge), edge)
            part = damping * part + restart[rows, :]
        ref[...] = part.astype(ref.dtype)


def final_kernel(chips, own, restart, *refs):
    parts, out = refs[:-1], refs[-1]
    _, _, core = place()
    topics = own.shape[1]
    for e in range(CORES):
        total = sum(ref[...].astype(jnp.float32) for ref in parts[e::CORES])
        lanes = pl.ds(pl.multiple_of(lax.rem(core + 1 - e, CORES) * topics, topics), topics)
        out[:, lanes] = (restart if e == 0 else own)[...] + damping * total


def from_col(value, chips, chip_step, core_step):
    route = [
        (x * CORES + c, (x + chip_step) % chips * CORES + (c + core_step) % CORES)
        for x in range(chips)
        for c in range(CORES)
    ]
    return lax.ppermute(value, "col", route)


def from_behind(value, steps, chips, distance, chip_step=0):
    columns = chips * CORES
    route = []
    for c in range(CORES):
        rows = cycle(c, steps)
        for i in range(steps):
            for x in range(chips):
                target = rows[(i + distance) % steps] * columns + (x + chip_step) % chips * CORES + c
                route.append((rows[i] * columns + x * CORES + c, target))
    return lax.ppermute(value, ("blk", "col"), route)


def body(tiles, tile_dest, tile_count, topic_seeds):
    slots, edge = tiles.shape[3], tiles.shape[4]
    steps, columns = lax.axis_size("blk"), lax.axis_size("col")
    chips = columns // CORES
    topics, seeds = topic_seeds.shape[0] // CORES, topic_seeds.shape[1]
    dests, sources, pair = columns * edge, steps * edge, CORES * edge
    groups = -(-steps // PACKED)
    scale = steps * columns * edge / seeds
    f32, bf16, i32 = jnp.float32, jnp.bfloat16, jnp.int32

    def shape(dtype, *dims):
        return jax.ShapeDtypeStruct(dims, dtype)

    def call(kernel, in_specs, outs, room, scratch=()):
        return pl.pallas_call(
            kernel,
            in_specs=in_specs,
            out_shape=outs,
            out_specs=[VMEM] * len(outs),
            scratch_shapes=scratch,
            compiler_params=pltpu.CompilerParams(vmem_limit_bytes=room),
        )

    matrix = 2 * dests * sources
    dense, send, seed_rows, restart_other = call(
        functools.partial(first_kernel, steps, columns, scale),
        [HBM] * 4,
        [
            shape(bf16, dests, sources),
            shape(bf16, dests, topics),
            shape(i32, seeds, topics),
            shape(f32, edge, topics),
        ],
        6 * MIB + 2 * matrix + 2 * steps * slots * edge * edge,
        [
            pltpu.VMEM((steps, slots, edge, edge), bf16),
            pltpu.SMEM(tile_dest.shape, i32),
            pltpu.SMEM(tile_count.shape, i32),
            pltpu.VMEM((seeds, CORES * topics), i32),
            pltpu.VMEM((2, dests + edge, edge), f32),
            pltpu.VMEM((seeds, topics), i32),
            pltpu.VMEM((groups, seeds, topics), i32),
            pltpu.VMEM((groups * edge // LOW, seeds, topics), i32),
            pltpu.SemaphoreType.DMA((steps,)),
            pltpu.SemaphoreType.DMA((3,)),
        ],
    )(*(pltpu.with_memory_space_constraint(a, pltpu.HBM) for a in (tiles, tile_dest, tile_count, topic_seeds.T)))
    recv = from_col(send, chips, 0, 1)
    keep, restart, restart_behind = call(
        functools.partial(keep_kernel, steps, columns, scale),
        [VMEM] * 2,
        [shape(f32, dests, topics)] + [shape(f32, pair, topics)] * 2,
        6 * MIB + 2 * matrix,
        [pltpu.VMEM((seeds, topics), i32), pltpu.VMEM((groups + 1, seeds, topics), i32)],
    )(dense, seed_rows)
    split = [shape(f32, pair, topics)] + [shape(bf16, pair, topics)] * chips
    parts = call(functools.partial(split_kernel, chips), [VMEM] * 2, split, 6 * MIB)(keep, recv)

    parts = list(parts)
    parts[0], tied = lax.optimization_barrier((parts[0], dense))
    other = from_col(tied, chips, 0, 1)
    far = steps - 2
    room = 6 * MIB + 2 * matrix
    for iteration in range(1, ITERS):
        mine, *sends = parts
        total = mine
        for d in range(1, chips):
            total = total + from_col(sends[d], chips, d, 0).astype(f32)
        behind = sum(from_behind(sends[d], steps, chips, 1, d).astype(f32) for d in range(chips))
        sent = (damping * total + restart).astype(bf16)
        sent_behind = (damping * behind + restart_behind).astype(bf16)
        arriving = [from_behind(sent, steps, chips, d) for d in range(steps - 1, 1, -1)]
        (near,) = call(functools.partial(near_kernel, steps), [VMEM] * 4, [shape(f32, dests, topics)], room)(
            dense, other, sent_behind, sent
        )
        if iteration < ITERS - 1:
            parts = call(
                functools.partial(step_kernel, steps, chips), [VMEM] * (3 + far), split, room
            )(dense, other, near, *arriving)
        else:
            away = call(
                functools.partial(last_kernel, steps, chips, 1),
                [VMEM] * (4 + far),
                [shape(bf16, edge, topics)] * (CORES * (chips - 1)),
                room,
            )(dense, other, near, restart, *arriving)
            home = call(
                functools.partial(last_kernel, steps, chips, 0),
                [VMEM] * (4 + far),
                [shape(f32, edge, topics), shape(bf16, edge, topics)],
                room,
            )(dense, other, near, restart, *arriving)
            parts = [*home, *away]
    own, core, *away = parts
    moved = [from_col(core, chips, 0, 1)]
    moved += [from_col(part, chips, 1 + i // CORES, i % CORES) for i, part in enumerate(away)]
    (out,) = call(
        functools.partial(final_kernel, chips),
        [VMEM] * (2 + len(moved)),
        [shape(f32, edge, CORES * topics)],
        4 * MIB,
    )(own, restart_other, *moved[:0:-1], moved[0])
    return out


def solution(mesh):
    return jax.shard_map(
        body,
        mesh=mesh,
        in_specs=(
            P(("parts", "blk"), "col", None, None, None, None),
            P(("parts", "blk"), "col", None, None),
            P(("parts", "blk"), "col", None),
            P("parts", None),
        ),
        out_specs=P(("parts", "blk", "col"), None),
        check_vma=False,
    )
```

```python
import functools

import jax
import jax.numpy as jnp
from jax import lax
from jax.experimental import pallas as pl
from jax.experimental.pallas import tpu as pltpu
from jax.sharding import PartitionSpec as P

ITERS = 3
CORES = 2
FIELD = 8
PACKED = 4
LOW = 32

damping = 0.85

VMEM = pl.BlockSpec(memory_space=pltpu.VMEM)
HBM = pl.BlockSpec(memory_space=pltpu.HBM)
MIB = 1 << 20


def place():
    col = lax.axis_index("col")
    return lax.axis_index("blk"), col // CORES, col % CORES


def cycle(core, steps):
    return list(range(steps)) if core == 0 else [0, *range(1, steps, 2), *range((steps - 1) // 2 * 2, 0, -2)]


def row_behind(row, core, steps, distance):
    place_out = jnp.where(row % 2 == 1, (row + 1) // 2, lax.rem(steps - row // 2, steps))
    at = lax.rem(jnp.where(core == 0, row, place_out) - distance + steps, steps)
    row_out = jnp.where(at <= steps // 2, jnp.maximum(2 * at - 1, 0), 2 * (steps - at))
    return jnp.where(core == 0, at, row_out)


def add_seeds(counts, ids, weights, first, last):
    rows = lax.broadcasted_iota(jnp.int32, counts[0].shape, 0)
    for j in range(first, last):
        hit = rows == ids[j : j + 1, :]
        counts = [c + jnp.where(hit, weights[g, j : j + 1, :], 0) for g, c in enumerate(counts)]
    return counts


def field(packed, index):
    return ((packed >> (FIELD * index)) & ((1 << FIELD) - 1)).astype(jnp.float32)


def source_weights(hosts, edge, steps, columns, row, col, weights):
    block = hosts >> (edge.bit_length() - 1)
    step = lax.rem(row - block // columns + steps, steps)
    mine = lax.rem(block, columns) == col
    one = 1 << (FIELD * lax.rem(step, PACKED))
    for g in range(-(-steps // PACKED)):
        weights[g] = jnp.where(mine & (step // PACKED == g), one, 0)
    return block


def source_rows(counts, scale, steps):
    parts = [scale * field(counts[s // PACKED], s % PACKED) for s in range(steps)]
    return jnp.concatenate(parts, axis=0).astype(jnp.bfloat16)


def first_kernel(
    steps, columns, scale, tiles_hbm, dest_hbm, count_hbm, seeds_hbm,
    dense, send, seed_rows, restart_other,
    tiles, dest, count, seeds, total, ids, weights, split, tile_sem, table_sem,
):
    slots, edge = tiles.shape[1], tiles.shape[2]
    topics = seeds.shape[1] // CORES
    row, chip, core = place()
    tables = [(seeds_hbm, seeds), (dest_hbm, dest), (count_hbm, count)]
    fetch_tables = [
        pltpu.make_async_copy(source, table, table_sem.at[i]) for i, (source, table) in enumerate(tables)
    ]
    fetch_tiles = [
        pltpu.make_async_copy(tiles_hbm.at[0, 0, s], tiles.at[s], tile_sem.at[s]) for s in range(steps)
    ]
    for fetch in fetch_tables + fetch_tiles:
        fetch.start()

    fetch_tables[0].wait()
    own, other = (
        seeds[:, pl.ds(pl.multiple_of(c * topics, topics), topics)] for c in (core, 1 - core)
    )
    seed_rows[...] = own
    ids[...] = other & (LOW - 1)
    source_weights(other, edge, steps, columns, row, chip * CORES + core, weights)
    high = (other & (edge - 1)) // LOW
    parts = edge // LOW
    for g in range(weights.shape[0]):
        for h in range(parts):
            split[g * parts + h] = jnp.where(high == h, weights[g], 0)
    counts = [jnp.zeros((LOW, topics), jnp.int32)] * split.shape[0]
    number, done = ids.shape[0], 0

    for fetch in fetch_tables[1:]:
        fetch.wait()
    for s in range(steps):
        upto = number * (s + 1) // steps
        counts = add_seeds(counts, ids, split, done, upto)
        done = upto
        fetch_tiles[s].wait()
        slot = s % total.shape[0]
        total[slot] = jnp.zeros(total.shape[1:], jnp.float32)
        for t in range(slots):
            block = jnp.where(t < count[0, 0, s], dest[0, 0, s, t], columns)
            rows = pl.ds(pl.multiple_of(block * edge, edge), edge)
            total[slot, rows, :] += tiles[s, t].astype(jnp.float32)
        dense[:, s * edge : (s + 1) * edge] = total[slot, : columns * edge, :].astype(jnp.bfloat16)

    counts = [jnp.concatenate(counts[g : g + parts], axis=0) for g in range(0, len(counts), parts)]
    restart_other[...] = (1.0 - damping) * (scale * field(counts[0], 0))
    restart = source_rows(counts, scale, steps)
    send[...] = jnp.dot(dense[...], restart, preferred_element_type=jnp.float32).astype(jnp.bfloat16)


def keep_kernel(steps, columns, scale, dense, seed_rows, keep, restart, restart_behind, ids, weights):
    edge = restart.shape[0] // CORES
    row, chip, core = place()
    hosts = seed_rows[...]
    ids[...] = hosts & (edge - 1)
    block = source_weights(hosts, edge, steps, columns, row, chip * CORES + core, weights)
    groups = weights.shape[0] - 1
    weights[groups] = jnp.zeros_like(hosts)
    for d in range(2):
        offset = block - row_behind(row, core, steps, d) * columns - chip * CORES
        for c in range(CORES):
            weights[groups] += jnp.where(offset == c, 1 << (FIELD * (d * CORES + c)), 0)
    counts = [jnp.zeros((edge, hosts.shape[1]), jnp.int32)] * (groups + 1)
    counts = add_seeds(counts, ids, weights, 0, ids.shape[0])
    for d, term in enumerate((restart, restart_behind)):
        for c in range(CORES):
            term[c * edge : (c + 1) * edge, :] = (1.0 - damping) * (
                scale * field(counts[groups], d * CORES + c)
            )
    rows = source_rows(counts, scale, steps)
    keep[...] = jnp.dot(dense[...], rows, preferred_element_type=jnp.float32)


def split_kernel(chips, keep, recv, mine, *sends):
    _, chip, _ = place()
    size = mine.shape[0]
    for d in range(chips):
        rows = pl.ds(pl.multiple_of(lax.rem(chip + d, chips) * size, size), size)
        part = keep[rows, :] + recv[rows, :].astype(jnp.float32)
        if d == 0:
            mine[...] = part
        sends[d][...] = part.astype(jnp.bfloat16)


def product(matrices, scores, rows, first, steps):
    row, _, core = place()
    edge = scores[0].shape[0] // CORES
    left, right = [], []
    for distance, score in enumerate(scores[::-1], first):
        step = lax.rem(row - row_behind(row, core, steps, distance) + steps, steps)
        for matrix, c in zip(matrices, (core, 1 - core)):
            left.append(matrix[rows, pl.ds(pl.multiple_of(step * edge, edge), edge)])
            right.append(score[pl.ds(pl.multiple_of(c * edge, edge), edge), :])
    return jnp.dot(
        jnp.concatenate(left, axis=1), jnp.concatenate(right, axis=0), preferred_element_type=jnp.float32
    )


def near_kernel(steps, own, other, *refs):
    scores, out = refs[:-1], refs[-1]
    out[...] = product((own, other), scores, slice(None), 0, steps)


def step_kernel(steps, chips, own, other, near, *refs):
    scores, mine, sends = refs[: -chips - 1], refs[-chips - 1], refs[-chips:]
    _, chip, _ = place()
    size = mine.shape[0]
    for d in [*range(1, chips), 0]:
        rows = pl.ds(pl.multiple_of(lax.rem(chip + d, chips) * size, size), size)
        part = near[rows, :] + product((own, other), scores, rows, steps - len(scores), steps)
        if d == 0:
            mine[...] = part
        sends[d][...] = part.astype(jnp.bfloat16)


def last_kernel(steps, chips, first, own, other, near, restart, *refs):
    scores, parts = refs[: steps - 2], refs[steps - 2 :]
    _, chip, core = place()
    edge = parts[0].shape[0]
    for i, ref in enumerate(parts):
        d, e = first + i // CORES, i % CORES
        block = lax.rem(chip + d, chips) * CORES + lax.rem(core + e, CORES)
        rows = pl.ds(pl.multiple_of(block * edge, edge), edge)
        part = near[rows, :] + product((own, other), scores, rows, steps - len(scores), steps)
        if d == e == 0:
            rows = pl.ds(pl.multiple_of(core * edge, edge), edge)
            part = damping * part + restart[rows, :]
        ref[...] = part.astype(ref.dtype)


def final_kernel(chips, own, restart, *refs):
    parts, out = [*refs[:-3], refs[-2], refs[-3]], refs[-1]
    _, _, core = place()
    topics = own.shape[1]
    for e in range(CORES):
        total = sum(ref[...].astype(jnp.float32) for ref in parts[e::CORES])
        lanes = pl.ds(pl.multiple_of(lax.rem(core + 1 - e, CORES) * topics, topics), topics)
        out[:, lanes] = (restart if e == 0 else own)[...] + damping * total


def from_col(value, chips, chip_step, core_step):
    route = [
        (x * CORES + c, (x + chip_step) % chips * CORES + (c + core_step) % CORES)
        for x in range(chips)
        for c in range(CORES)
    ]
    return lax.ppermute(value, "col", route)


def from_behind(value, steps, chips, distance, chip_step=0):
    columns = chips * CORES
    route = []
    for c in range(CORES):
        rows = cycle(c, steps)
        for i in range(steps):
            for x in range(chips):
                target = rows[(i + distance) % steps] * columns + (x + chip_step) % chips * CORES + c
                route.append((rows[i] * columns + x * CORES + c, target))
    return lax.ppermute(value, ("blk", "col"), route)


def body(tiles, tile_dest, tile_count, topic_seeds):
    slots, edge = tiles.shape[3], tiles.shape[4]
    steps, columns = lax.axis_size("blk"), lax.axis_size("col")
    chips = columns // CORES
    topics, seeds = topic_seeds.shape[0] // CORES, topic_seeds.shape[1]
    dests, sources, pair = columns * edge, steps * edge, CORES * edge
    groups = -(-steps // PACKED)
    scale = steps * columns * edge / seeds
    f32, bf16, i32 = jnp.float32, jnp.bfloat16, jnp.int32

    def shape(dtype, *dims):
        return jax.ShapeDtypeStruct(dims, dtype)

    def call(kernel, in_specs, outs, room, scratch=()):
        return pl.pallas_call(
            kernel,
            in_specs=in_specs,
            out_shape=outs,
            out_specs=[VMEM] * len(outs),
            scratch_shapes=scratch,
            compiler_params=pltpu.CompilerParams(vmem_limit_bytes=room),
        )

    matrix = 2 * dests * sources
    dense, send, seed_rows, restart_other = call(
        functools.partial(first_kernel, steps, columns, scale),
        [HBM] * 4,
        [
            shape(bf16, dests, sources),
            shape(bf16, dests, topics),
            shape(i32, seeds, topics),
            shape(f32, edge, topics),
        ],
        6 * MIB + 2 * matrix + 2 * steps * slots * edge * edge,
        [
            pltpu.VMEM((steps, slots, edge, edge), bf16),
            pltpu.SMEM(tile_dest.shape, i32),
            pltpu.SMEM(tile_count.shape, i32),
            pltpu.VMEM((seeds, CORES * topics), i32),
            pltpu.VMEM((2, dests + edge, edge), f32),
            pltpu.VMEM((seeds, topics), i32),
            pltpu.VMEM((groups, seeds, topics), i32),
            pltpu.VMEM((groups * edge // LOW, seeds, topics), i32),
            pltpu.SemaphoreType.DMA((steps,)),
            pltpu.SemaphoreType.DMA((3,)),
        ],
    )(*(pltpu.with_memory_space_constraint(a, pltpu.HBM) for a in (tiles, tile_dest, tile_count, topic_seeds.T)))
    recv = from_col(send, chips, 0, 1)
    keep, restart, restart_behind = call(
        functools.partial(keep_kernel, steps, columns, scale),
        [VMEM] * 2,
        [shape(f32, dests, topics)] + [shape(f32, pair, topics)] * 2,
        6 * MIB + 2 * matrix,
        [pltpu.VMEM((seeds, topics), i32), pltpu.VMEM((groups + 1, seeds, topics), i32)],
    )(dense, seed_rows)
    split = [shape(f32, pair, topics)] + [shape(bf16, pair, topics)] * chips
    parts = call(functools.partial(split_kernel, chips), [VMEM] * 2, split, 6 * MIB)(keep, recv)

    parts = list(parts)
    parts[0], tied = lax.optimization_barrier((parts[0], dense))
    other = from_col(tied, chips, 0, 1)
    far = steps - 2
    room = 6 * MIB + 2 * matrix
    for iteration in range(1, ITERS):
        mine, *sends = parts
        total = mine
        for d in range(1, chips):
            total = total + from_col(sends[d], chips, d, 0).astype(f32)
        behind = sum(from_behind(sends[d], steps, chips, 1, d).astype(f32) for d in range(chips))
        sent = (damping * total + restart).astype(bf16)
        sent_behind = (damping * behind + restart_behind).astype(bf16)
        arriving = [from_behind(sent, steps, chips, d) for d in range(steps - 1, 1, -1)]
        (near,) = call(functools.partial(near_kernel, steps), [VMEM] * 4, [shape(f32, dests, topics)], room)(
            dense, other, sent_behind, sent
        )
        if iteration < ITERS - 1:
            parts = call(
                functools.partial(step_kernel, steps, chips), [VMEM] * (3 + far), split, room
            )(dense, other, near, *arriving)
        else:
            away = call(
                functools.partial(last_kernel, steps, chips, 1),
                [VMEM] * (4 + far),
                [shape(bf16, edge, topics)] * (CORES * (chips - 1)),
                room,
            )(dense, other, near, restart, *arriving)
            home = call(
                functools.partial(last_kernel, steps, chips, 0),
                [VMEM] * (4 + far),
                [shape(f32, edge, topics), shape(bf16, edge, topics)],
                room,
            )(dense, other, near, restart, *arriving)
            parts = [*home, *away]
    own, core, *away = parts
    moved = [from_col(core, chips, 0, 1)]
    moved += [from_col(part, chips, 1 + i // CORES, i % CORES) for i, part in enumerate(away)]
    (out,) = call(
        functools.partial(final_kernel, chips),
        [VMEM] * (2 + len(moved)),
        [shape(f32, edge, CORES * topics)],
        4 * MIB,
    )(own, restart_other, *moved[:1:-1], moved[0], moved[1])
    return out


def solution(mesh):
    return jax.shard_map(
        body,
        mesh=mesh,
        in_specs=(
            P(("parts", "blk"), "col", None, None, None, None),
            P(("parts", "blk"), "col", None, None),
            P(("parts", "blk"), "col", None),
            P("parts", None),
        ),
        out_specs=P(("parts", "blk", "col"), None),
        check_vma=False,
    )
```
